256 devices in a mesh: dp: 32 (over x, y, core), mp: 8 (over z).
Axes of the slice: x: 4, y: 4, z: 8, core: 2. Of those that a mesh axis runs over, the one named last changes fastest.
Arguments:
- tokens: bfloat16 [32768, 4096], P(('dp', 'mp')), may hold values from -200 to 200
- w_query: bfloat16 [4096, 2048], P(None, 'mp'), may hold values from -0.09375 to 0.09375
- w_key: bfloat16 [896, 2048], P(None, 'mp'), may hold values from -0.1875 to 0.1875
- w_value: bfloat16 [896, 2048], P(None, 'mp'), may hold values from -0.1875 to 0.1875
- w_out: bfloat16 [2048, 4096], P('mp'), may hold values from -0.375 to 0.375
- encoded: bfloat16 [512, 128, 896], P('dp'), may hold values from -6 to 6
- nbr_shard: int32 [512, 2], P('dp'), may hold values from 0 to 31, as said below
- nbr_row: int32 [512, 2], P('dp'), may hold values from 0 to 15
Outputs:
- mixed: bfloat16 [32768, 4096], P(('dp', 'mp'))
The draws below stay inside these ranges and needn't reach their ends.
Inputs may be any that keep to these rules, and one draw needn't show every extreme that they name: `nbr_shard`: the 32 neighbours of one sequence's spans name each cache shard either never or exactly 2 times; how often a shard is named over all sequences differs widely between shards.
All inputs are finite; a program needn't handle non-finite values.
Results may differ from the reference program's by a relative error of at most 0.019.
The reference program's roundings to bfloat16 on the way count: a program that leaves them out, or rounds other values in their place, can miss the bound.
Values may be sent and summed in bfloat16 or wider, within the bound.
A program may use at most 128 MiB of HBM per device.

```python
import math
import jax
import jax.numpy as jnp
from jax import lax

D = 4096
HEADS = 16
HD = 128
ENC = 896
SPAN = 64
NLEN = 128
NBR = 2
TOK_DEV = 1024
CACHE_DEV = 16
SPANS_DEV = 16
SPANS = 512
TOKENS = 32768
ENTRIES = 512
CAP = 2
HEADS_GROUP = 2
N_DP = 32
N_MP = 8


def retrieval_lists(key):
    fetches = SPANS_DEV * NBR
    distinct = fetches // CAP
    heat_key, pick_key, order_key, row_key = jax.random.split(key, 4)
    heat = jax.random.randint(heat_key, (N_DP,), 0, 4)
    favour = jnp.left_shift(jnp.ones((N_DP,), jnp.int32), heat)
    noise = jax.random.randint(pick_key, (N_DP, N_DP), 1, 2 ** 20)
    score = noise * favour[None, :] * 64 + jnp.arange(N_DP, dtype=jnp.int32)[None, :]
    picked = lax.top_k(score, distinct)[1].astype(jnp.int32)
    shard_list = jnp.tile(picked, (1, CAP))
    mixing = jax.random.randint(order_key, (N_DP, fetches), 0, 2 ** 20) * fetches + jnp.arange(fetches, dtype=jnp.int32)[None, :]
    placing = jnp.argsort(mixing, axis=1)
    shard_list = jnp.take_along_axis(shard_list, placing, axis=1)
    row_list = jax.random.randint(row_key, (N_DP, fetches), 0, CACHE_DEV)
    return (shard_list.reshape(SPANS, NBR).astype(jnp.int32), row_list.reshape(SPANS, NBR).astype(jnp.int32))


def draw_nbr_shard(key, part):
    return retrieval_lists(key)[0]


def draw_nbr_row(key, part):
    return retrieval_lists(key)[1]


def draw_tokens(key, part):
    key = jax.random.fold_in(key, 11)
    values = jnp.clip(jax.random.normal(key, (TOKENS, D), jnp.float32), -4.0, 4.0)
    return values.astype(jnp.bfloat16)


def block_levels(stream_key, extent, cuts, least, high):
    gain, own = 1.0, jax.random.fold_in(stream_key, 6)
    for dim, blocks in cuts:
        heights = jnp.exp(jax.random.uniform(jax.random.fold_in(own, dim), (blocks,), jnp.float32, least / len(cuts), high / len(cuts)))
        gain = gain * jnp.repeat(heights, extent[dim] // blocks).reshape([-1 if axis == dim else 1 for axis in range(len(extent))])
    return gain


def centred(stream_key, shape, scale, reach, cuts=(), kind=jnp.bfloat16):
    values = scale * jax.random.normal(stream_key, shape, jnp.float32)
    if cuts:
        values = values * block_levels(stream_key, shape, cuts, -0.22, 0.18)
    return jnp.clip(values, -reach, reach).astype(kind)


def setup_inputs(seed: int = 0) -> dict:
    arg_keys = jax.random.split(jax.random.key(seed), 9)
    return {
        "tokens": draw_tokens(jax.random.fold_in(arg_keys[8], 71), 0),
        "w_query": centred(arg_keys[1], (D, HEADS * HD), D ** -0.5, 0.09375, ((1, 8),)),
        "w_key": centred(arg_keys[2], (ENC, HEADS * HD), ENC ** -0.5, 0.1875, ((1, 8),)),
        "w_value": centred(arg_keys[3], (ENC, HEADS * HD), ENC ** -0.5, 0.1875, ((1, 8),)),
        "w_out": centred(arg_keys[4], (HEADS * HD, D), (HEADS * HD // 8) ** -0.5, 0.375, ((0, 8),)),
        "encoded": centred(arg_keys[5], (ENTRIES, NLEN, ENC), 1.0, 6.0, ((0, 32),)),
        "nbr_shard": draw_nbr_shard(jax.random.fold_in(arg_keys[8], 71), 0),
        "nbr_row": draw_nbr_row(jax.random.fold_in(arg_keys[8], 71), 0),
    }


def settled(values):
    return lax.optimization_barrier(values)

def shifted_blocks(queries):
    row_width = queries.shape[1]
    zero_tail = jnp.zeros((SPAN - 1, row_width), queries.dtype)
    shifted = jnp.concatenate([queries[SPAN - 1:], zero_tail], axis=0)
    return shifted.reshape(queries.shape[0] // SPAN, SPAN, row_width)

def attend_block(query_blocks, key_rows, value_rows):
    block_count = query_blocks.shape[0]
    head_count = query_blocks.shape[2] // HD
    query_heads = settled(query_blocks).astype(jnp.float32).reshape(block_count, SPAN, head_count, HD)
    key_heads = settled(key_rows).astype(jnp.float32).reshape(block_count, NLEN, head_count, HD)
    value_heads = settled(value_rows).astype(jnp.float32).reshape(block_count, NLEN, head_count, HD)
    scores = jnp.einsum('bqhd,bkhd->bhqk', query_heads, key_heads) * jnp.float32(1.0 / math.sqrt(HD))
    peak_score = lax.optimization_barrier(jnp.max(scores, axis=3, keepdims=True))
    exponent = jnp.exp(scores - peak_score)
    totals = lax.optimization_barrier(jnp.sum(exponent, axis=3, keepdims=True))
    weights = settled(exponent.astype(jnp.bfloat16)).astype(jnp.float32)
    summed = jnp.einsum('bhqk,bkhd->bqhd', weights, value_heads)
    scaled = summed / jnp.transpose(totals, (0, 2, 1, 3))
    partial_value = scaled.astype(jnp.bfloat16).reshape(block_count, SPAN, head_count * HD)
    spread = (peak_score + jnp.log(totals))[..., 0]
    return (partial_value, spread)

def combine(partial_value, spread):
    span_count = partial_value.shape[0] // NBR
    head_count = spread.shape[1]
    spread = spread.reshape(span_count, NBR, head_count, SPAN)
    top_scale = lax.optimization_barrier(jnp.max(spread, axis=1, keepdims=True))
    shares = jnp.exp(spread - top_scale)
    shares = shares / lax.optimization_barrier(jnp.sum(shares, axis=1, keepdims=True))
    shares = jnp.transpose(shares, (0, 1, 3, 2))[..., None]
    pieces = settled(partial_value).astype(jnp.float32).reshape(span_count, NBR, SPAN, head_count, HD)
    merged = lax.optimization_barrier(jnp.sum(pieces * shares, axis=1))
    return merged.astype(jnp.bfloat16).reshape(span_count * SPAN, head_count * HD)

def unshifted(attention):
    zero_head = jnp.zeros((SPAN - 1, attention.shape[1]), attention.dtype)
    return jnp.concatenate([zero_head, attention[:attention.shape[0] - (SPAN - 1)]], axis=0)

def reference(tokens, w_query, w_key, w_value, w_out, encoded, nbr_shard, nbr_row):
    queries = jnp.dot(tokens, w_query, preferred_element_type=jnp.float32).astype(jnp.bfloat16)
    flat_cache = encoded.reshape(-1, ENC)
    cache_keys = jnp.dot(flat_cache, w_key, preferred_element_type=jnp.float32).astype(jnp.bfloat16).reshape(-1, NLEN, HEADS * HD)
    cache_values = jnp.dot(flat_cache, w_value, preferred_element_type=jnp.float32).astype(jnp.bfloat16).reshape(-1, NLEN, HEADS * HD)
    entry_ids = (nbr_shard * CACHE_DEV + nbr_row).astype(jnp.int32)

    def one_sequence(sequence):
        seq_queries = lax.dynamic_slice_in_dim(queries, sequence * TOK_DEV, TOK_DEV, 0)
        blocks = shifted_blocks(seq_queries)
        picked = lax.dynamic_slice_in_dim(entry_ids, sequence * SPANS_DEV, SPANS_DEV, 0).reshape(SPANS_DEV * NBR)
        partial_value, spread = attend_block(jnp.repeat(blocks, NBR, axis=0), jnp.take(cache_keys, picked, axis=0), jnp.take(cache_values, picked, axis=0))
        return unshifted(combine(partial_value, spread))
    attended = lax.map(one_sequence, jnp.arange(N_DP, dtype=jnp.int32)).reshape(TOKENS, HEADS * HD)
    group_width = HEADS_GROUP * HD
    summed = jnp.zeros((TOKENS, D), jnp.float32)
    for group in range(N_MP):
        lower = group * group_width
        group_term = jnp.dot(attended[:, lower:lower + group_width], w_out[lower:lower + group_width], preferred_element_type=jnp.float32).astype(jnp.bfloat16)
        summed = summed + settled(group_term).astype(jnp.float32)
    return summed.astype(jnp.bfloat16)
```

```python
import functools
import math

import jax
import jax.numpy as jnp
from jax import lax
from jax.experimental import pallas as pl
from jax.experimental.pallas import tpu as pltpu
from jax.sharding import PartitionSpec as P

MESH = pl.DeviceIdType.MESH
BF = jnp.bfloat16
F32 = jnp.float32
HD = 128
SPAN = 64
D = 4096
ENC = 896
TOK = 128
NX = 4
NZ = 8
NP = 32
ROWS = 16
QZ = 1024
QU = (D - QZ) // 16
OU = D // 16
SLOTS = ((1, 0), (1, 1), (2, 0), (2, 1), (3, 0), (3, 1), (0, 1))
OUT_CHUNK = 512


def kernel(
    tok, wq, wk, wv, wo, enc, ask, slot, out,
    tokv, ttail, wqb, wkb, wvb, wob, band, ask_r, ask_s, send_e, recv_e, send_z, encz,
    qb, kb, vb, att, att0, acc, t_send, t_recv, r_own, r_in,
    l_sem, sz, rz, sx, rx, sa, ra, se, re, s2, r2, st, rt, sf, rf,
):
    d = lax.axis_index("dp")
    z = lax.axis_index("mp")
    x = d // 8
    y = lax.rem(d // 2, 4)
    c = lax.rem(d, 2)
    other = (d + 1 - 2 * c, z)
    zdn = (d, lax.rem(z + 7, NZ))
    zup = (d, lax.rem(z + 1, NZ))
    odn = (other[0], zdn[1])
    oup = (other[0], zup[1])

    def plane(px, py):
        return (px * 8 + py * 2 + c, z)

    ring = {
        "x": (plane(lax.rem(x + 1, 4), y), plane(lax.rem(x + 3, 4), y)),
        "y": (plane(x, lax.rem(y + 1, 4)), plane(x, lax.rem(y + 3, 4))),
    }
    cs = pl.ds(pl.multiple_of(c * HD, HD), HD)

    def remote(src, dst, ssem, rsem, dev):
        return pltpu.make_async_remote_copy(
            src_ref=src, dst_ref=dst, send_sem=ssem, recv_sem=rsem, device_id=dev, device_id_type=MESH
        )

    half0 = pl.ds(0, HD)
    local = [
        pltpu.make_async_copy(enc.at[:, pl.ds(pl.multiple_of(z * ROWS, ROWS), ROWS), :], band, l_sem.at[0]),
        pltpu.make_async_copy(tok, tokv.at[pl.ds(0, TOK)], l_sem.at[1]),
        pltpu.make_async_copy(wq.at[:, cs], wqb.at[0, :, half0], l_sem.at[2]),
        pltpu.make_async_copy(wk.at[:, cs], wkb.at[0, :, half0], l_sem.at[3]),
        pltpu.make_async_copy(wv.at[:, cs], wvb.at[0, :, half0], l_sem.at[4]),
        pltpu.make_async_copy(wo.at[cs, :], wob.at[0, half0, :], l_sem.at[5]),
    ]
    for copy in local:
        copy.start()

    bar = pltpu.get_barrier_semaphore()

    def greet_plane(k, carry):
        pl.semaphore_signal(bar, inc=1, device_id=(lax.rem(d + k, NP), z), device_id_type=MESH)
        return carry

    def greet_z(k, carry):
        pl.semaphore_signal(bar, inc=1, device_id=(d, lax.rem(z + k, NZ)), device_id_type=MESH)
        return carry

    lax.fori_loop(1, NP, greet_plane, 0)
    lax.fori_loop(1, NZ, greet_z, 0)
    pl.semaphore_signal(bar, inc=1, device_id=odn, device_id_type=MESH)
    pl.semaphore_signal(bar, inc=1, device_id=oup, device_id_type=MESH)
    pl.semaphore_wait(bar, NP - 1 + NZ - 1 + 2)

    qi = y * 4 + x
    oi = x * 4 + y

    def q_at(sl, start, size):
        if sl is None:
            return wq.at[pl.ds(start, size), cs]
        return wqb.at[sl[0], pl.ds(start, size), pl.ds(sl[1] * HD, HD)]

    def o_at(sl, start, size):
        if sl is None:
            return wo.at[cs, pl.ds(start, size)]
        return wob.at[sl[0], pl.ds(sl[1] * HD, HD), pl.ds(start, size)]

    def kv_at(arg, buf, sl):
        if sl is None:
            return arg.at[:, cs]
        return buf.at[sl[0], :, pl.ds(sl[1] * HD, HD)]

    started = []

    def go(copy):
        copy.start()
        started.append(copy)
        return copy

    def flush(keep):
        while len(started) > keep:
            started.pop(0).wait_send()

    zc = {}

    def z_copy(way, k, part):
        src_sl = None if k == 1 else (k - 1, way)
        dst_sl = (k, way) if k < 4 else (0, 1)
        if part == 0:
            start = pl.multiple_of(QZ + qi * QU + (QU // 2 if k == 4 and way else 0), 16)
            size = QU // 2 if k == 4 else QU
            src, dst = q_at(src_sl, start, size), q_at(dst_sl, start, size)
        elif part == 1:
            start = pl.multiple_of(oi * OU + (OU // 2 if k == 4 and way else 0), 128)
            size = OU // 2 if k == 4 else OU
            src, dst = o_at(src_sl, start, size), o_at(dst_sl, start, size)
        elif part == 2:
            src, dst = kv_at(wk, wkb, src_sl), kv_at(wk, wkb, dst_sl)
        elif part == 3:
            src, dst = kv_at(wv, wvb, src_sl), kv_at(wv, wvb, dst_sl)
        else:
            start = QZ // 2 if k == 4 and way else 0
            size = QZ // 2 if k == 4 else QZ
            src, dst = q_at(src_sl, start, size), q_at(dst_sl, start, size)
        zc[way, k, part] = go(
            remote(src, dst, sz.at[way, k - 1, part], rz.at[way, k - 1, part], zup if way else zdn)
        )

    def z_parts(way, k, parts):
        return [p for p in parts if not (k == 4 and p == (2 if way else 3))]

    def z_start(k, parts):
        for p in parts:
            for way in (0, 1):
                if p in z_parts(way, k, parts):
                    z_copy(way, k, p)

    def z_wait(k, parts):
        for p in parts:
            for way in (0, 1):
                if p in z_parts(way, k, parts):
                    zc[way, k, p].wait_recv()

    SL, BULK = (0, 1), (2, 3, 4)

    xc = {}

    def view(arr, sl, start, size):
        if arr == 0:
            return q_at(sl, pl.multiple_of(QZ + start, 16), size)
        return o_at(sl, pl.multiple_of(start, 128), size)

    unit = (QU, OU)
    first = (x, y)
    second = (y, x)
    axes = (("x", "y"), ("y", "x"))

    def x_start(t, phase):
        sl = SLOTS[t]
        for arr in (0, 1):
            u, i1, i2 = unit[arr], first[arr], second[arr]
            up, dn = ring[axes[arr][phase // 2]]
            if phase == 0:
                spans = [((i2 * 4 + i1) * u, u)] * 2
            elif phase == 1:
                spans = [
                    ((i2 * 4 + lax.rem(i1 + 3, 4)) * u, u // 2),
                    ((i2 * 4 + lax.rem(i1 + 1, 4)) * u + u // 2, u // 2),
                ]
            elif phase == 2:
                spans = [(i2 * 4 * u, 4 * u)] * 2
            else:
                spans = [
                    (lax.rem(i2 + 3, 4) * 4 * u, 2 * u),
                    (lax.rem(i2 + 1, 4) * 4 * u + 2 * u, 2 * u),
                ]
            for way, dev in enumerate((up, dn)):
                ref = view(arr, sl, *spans[way])
                xc[t, phase, arr, way] = go(
                    remote(ref, ref, sx.at[arr, t, phase * 2 + way], rx.at[arr, t, phase * 2 + way], dev)
                )

    def x_wait(t, phase):
        for arr in (0, 1):
            for way in (0, 1):
                xc[t, phase, arr, way].wait_recv()

    def step(t, phase):
        x_wait(t, phase)
        if phase < 3:
            x_start(t, phase + 1)

    z_start(1, SL)
    last16 = pl.ds(TOK - 16, 16)
    tail_in = go(remote(tok.at[last16], ttail, st.at[0], rt.at[0], zup))

    def ask_copy(k):
        p = lax.rem(d + k, NP)
        return remote(ask.at[p], ask_r.at[d], sa.at[k], ra.at[k], (p, z))

    def each(n, f):
        def body(k, carry):
            f(k)
            return carry

        lax.fori_loop(1, n, body, 0)

    each(NP, lambda k: ask_copy(k).start())
    z_start(1, BULK)
    ask_r[pl.ds(d, 1)] = ask[pl.ds(d, 1)]
    each(NP, lambda k: ask_copy(k).wait_recv())
    to_smem = pltpu.make_async_copy(ask_r, ask_s, l_sem.at[6])
    to_smem.start()
    to_smem.wait()
    local[0].wait()

    def pick(s, carry):
        for j in range(2):
            send_e[s, j] = band[ask_s[s, 0, j]]
        return carry

    lax.fori_loop(0, NP, pick, 0)

    def e1_copy(k):
        p = lax.rem(d + k, NP)
        return remote(send_e.at[p], recv_e.at[pl.ds(2 * d, 2)], se.at[k], re.at[k], (p, z))

    each(NP, lambda k: e1_copy(k).start())
    recv_e[pl.ds(2 * d, 2)] = send_e[d]

    local[1].wait()
    tail_in.wait_recv()
    is15 = lax.broadcasted_iota(jnp.int32, (16, D), 0) == 15
    tokv[TOK - 16 : TOK, :] = jnp.where(is15, ttail[...], tokv[TOK - 16 : TOK, :])
    tok_x = go(remote(tokv.at[pl.ds(0, TOK)], tokv.at[pl.ds(TOK, TOK)], st.at[1], rt.at[1], other))

    for k in range(1, 5):
        z_wait(k, SL)
        if k < 4:
            z_start(k + 1, SL)
            x_start(2 * k - 2, 0)
            x_start(2 * k - 1, 0)
        else:
            x_start(6, 0)

    def project(pair, half):
        lanes = pl.ds(0, 256) if half is None else pl.ds(half * HD, HD)
        width = 256 if half is None else HD

        def body(k, total):
            start = pl.multiple_of(k * 512, 512)
            return total + jnp.dot(
                tokv[:, pl.ds(start, 512)], wqb[pair, pl.ds(start, 512), lanes], preferred_element_type=F32
            )

        total = lax.fori_loop(0, D // 512, body, jnp.zeros((2 * TOK, width), F32))
        qb[:, lanes] = total.astype(BF)

    def keys_values(pair, half):
        lanes = pl.ds(0, 256) if half is None else pl.ds(half * HD, HD)

        def body(u, carry):
            rows = encz[pl.ds(2 * u, 2)].reshape(256, ENC)
            kb[u, :, lanes] = jnp.dot(rows, wkb[pair, :, lanes], preferred_element_type=F32).astype(BF)
            vb[u, :, lanes] = jnp.dot(rows, wvb[pair, :, lanes], preferred_element_type=F32).astype(BF)
            return carry

        lax.fori_loop(0, 4, body, 0)

    row_id = lax.broadcasted_iota(jnp.int32, (TOK, 256), 0)
    in_b = jnp.logical_and(row_id >= SPAN - 1, row_id < TOK - 1)
    blank = jnp.logical_and(lax.broadcasted_iota(jnp.int32, (TOK, HD), 0) < SPAN - 1, z == 0)

    def attend(half, dst):
        halves = (0, 1) if half is None else (half,)
        for s in range(2):
            for h in halves:
                lanes = pl.ds(h * HD, HD)
                q = qb[s * TOK : (s + 1) * TOK, lanes]
                ka, kb_ = kb[2 * s, :, lanes], kb[2 * s + 1, :, lanes]
                dims = (((1,), (1,)), ((), ()))
                sa_ = lax.dot_general(q, ka, dims, preferred_element_type=F32)
                sb_ = lax.dot_general(q, kb_, dims, preferred_element_type=F32)
                scores = jnp.where(in_b, sb_, sa_) * F32(1.0 / math.sqrt(HD))
                peak = jnp.max(scores, axis=1, keepdims=True)
                e = jnp.exp(scores - peak)
                total = jnp.sum(e, axis=1, keepdims=True)
                wa = jnp.where(in_b, 0.0, e).astype(BF)
                wb = jnp.where(in_b, e, 0.0).astype(BF)
                o = jnp.dot(wa, vb[2 * s, :, lanes], preferred_element_type=F32)
                o = o + jnp.dot(wb, vb[2 * s + 1, :, lanes], preferred_element_type=F32)
                o = jnp.where(blank, 0.0, o / total)
                dst[s * TOK : (s + 1) * TOK, lanes] = o.astype(BF)

    def add_out(pair, is_first):
        def body(k, carry):
            cols = pl.ds(pl.multiple_of(k * OUT_CHUNK, OUT_CHUNK), OUT_CHUNK)
            term = jnp.dot(att[...], wob[pair, :, cols], preferred_element_type=F32)
            acc[:, cols] = term if is_first else acc[:, cols] + term
            return carry

        lax.fori_loop(0, D // OUT_CHUNK, body, 0)

    step(0, 0)
    step(1, 0)
    step(0, 1)
    step(1, 1)
    tok_x.wait_recv()
    local[2].wait()
    project(0, 0)
    step(2, 0)
    step(3, 0)
    each(NP, lambda k: e1_copy(k).wait_recv())

    def pick_z(mz, carry):
        fa = lax.rem(4 * mz + 30, 32)
        for i in range(2):
            send_z[mz, i] = recv_e[slot[0, fa + i]]
            send_z[mz, 2 + i] = recv_e[slot[0, 4 * mz + i]]
        return carry

    lax.fori_loop(0, NZ, pick_z, 0)
    my_rows = pl.ds(pl.multiple_of(z * ROWS, ROWS), ROWS)

    def e2_copy(k):
        p = lax.rem(z + k, NZ)
        return remote(send_z.at[p], encz.at[pl.ds(0, 4), my_rows, :], s2.at[k], r2.at[k], (d, p))

    each(NZ, lambda k: e2_copy(k).start())
    encz[pl.ds(0, 4), my_rows, :] = send_z[z]
    step(0, 2)
    step(1, 2)
    step(2, 1)
    step(3, 1)
    z_wait(1, BULK)
    z_start(2, BULK)
    step(4, 0)
    step(5, 0)
    step(6, 0)
    each(NZ, lambda k: e2_copy(k).wait_recv())
    enc_x = go(remote(encz.at[pl.ds(0, 4)], encz.at[pl.ds(4, 4)], st.at[2], rt.at[2], other))
    flush(40)
    local[3].wait()
    local[4].wait()
    local[5].wait()
    enc_x.wait_recv()
    keys_values(0, 0)
    attend(0, att0)
    step(0, 3)
    step(1, 3)
    step(2, 2)
    step(3, 2)
    step(4, 1)
    step(5, 1)
    project(1, None)
    keys_values(1, None)
    z_wait(2, BULK)
    z_start(3, BULK)
    attend(None, att)
    add_out(1, True)
    flush(30)
    step(2, 3)
    step(3, 3)
    step(4, 2)
    step(5, 2)
    step(6, 1)
    project(2, None)
    keys_values(2, None)
    z_wait(3, BULK)
    z_start(4, BULK)
    attend(None, att)
    add_out(2, False)
    flush(30)
    step(4, 3)
    step(5, 3)
    step(6, 2)
    project(3, None)
    keys_values(3, None)
    attend(None, att)
    add_out(3, False)
    each(NP, lambda k: ask_copy(k).wait_send())
    each(NP, lambda k: e1_copy(k).wait_send())
    each(NZ, lambda k: e2_copy(k).wait_send())
    flush(4)
    step(6, 3)
    z_wait(4, BULK)
    project(0, 1)
    keys_values(0, 1)
    attend(1, att0)
    flush(0)

    def t_copy(k):
        cols = pl.ds(pl.multiple_of(k * OUT_CHUNK, OUT_CHUNK), OUT_CHUNK)
        return remote(t_send.at[:, cols], t_recv.at[:, cols], sf.at[k], rf.at[k], other)

    def last(k, carry):
        cols = pl.ds(pl.multiple_of(k * OUT_CHUNK, OUT_CHUNK), OUT_CHUNK)
        term = acc[:, cols] + jnp.dot(att0[...], wob[0, :, cols], preferred_element_type=F32)
        acc[0:TOK, cols] = term[:TOK]
        t_send[:, cols] = term[TOK:].astype(BF)
        r_own[:, cols] = term[TOK - 16 : TOK].astype(BF)
        t_copy(k).start()
        return carry

    n = D // OUT_CHUNK
    lax.fori_loop(0, n, last, 0)
    row_a = remote(r_own, r_in.at[0], sf.at[n], rf.at[n], zdn)
    row_b = remote(t_send.at[last16], r_in.at[1], sf.at[n + 1], rf.at[n + 1], odn)
    row_a.start()
    row_b.start()

    def finish(k, carry):
        cols = pl.ds(pl.multiple_of(k * OUT_CHUNK, OUT_CHUNK), OUT_CHUNK)
        t_copy(k).wait()
        out[:, cols] = (acc[0:TOK, cols] + t_recv[:, cols].astype(F32)).astype(BF)
        return carry

    lax.fori_loop(0, n, finish, 0)
    row_a.wait()
    row_b.wait()
    fixed = (r_in[0].astype(F32) + r_in[1].astype(F32)).astype(BF)
    out[TOK - 16 : TOK, :] = jnp.where(is15, fixed, out[TOK - 16 : TOK, :])


def fused(tokens, w_query, w_key, w_value, w_out, encoded, ask, slot):
    any_ = pl.BlockSpec(memory_space=pl.ANY)
    vmem = pl.BlockSpec(memory_space=pltpu.VMEM)
    smem = pl.BlockSpec(memory_space=pltpu.SMEM)
    dma = pltpu.SemaphoreType.DMA
    V = pltpu.VMEM
    n = D // OUT_CHUNK
    return pl.pallas_call(
        kernel,
        out_shape=jax.ShapeDtypeStruct((TOK, D), BF),
        in_specs=[any_] * 6 + [vmem, smem],
        out_specs=vmem,
        scratch_shapes=[
            V((2 * TOK, D), BF),
            V((16, D), BF),
            V((4, D, 256), BF),
            V((4, ENC, 256), BF),
            V((4, ENC, 256), BF),
            V((4, 256, D), BF),
            V((16, ROWS, ENC), BF),
            V((NP, 1, 128), jnp.int32),
            pltpu.SMEM((NP, 1, 128), jnp.int32),
            V((NP, 2, ROWS, ENC), BF),
            V((2 * NP, ROWS, ENC), BF),
            V((NZ, 4, ROWS, ENC), BF),
            V((8, 128, ENC), BF),
            V((2 * TOK, 256), BF),
            V((4, 256, 256), BF),
            V((4, 256, 256), BF),
            V((2 * TOK, 256), BF),
            V((2 * TOK, 256), BF),
            V((2 * TOK, D), F32),
            V((TOK, D), BF),
            V((TOK, D), BF),
            V((16, D), BF),
            V((2, 16, D), BF),
            dma((7,)),
            dma((2, 4, 5)),
            dma((2, 4, 5)),
            dma((2, 7, 8)),
            dma((2, 7, 8)),
            dma((NP,)),
            dma((NP,)),
            dma((NP,)),
            dma((NP,)),
            dma((NZ,)),
            dma((NZ,)),
            dma((3,)),
            dma((3,)),
            dma((n + 2,)),
            dma((n + 2,)),
        ],
        compiler_params=pltpu.CompilerParams(
            collective_id=0, has_side_effects=True, vmem_limit_bytes=56 * 1024 * 1024
        ),
    )(tokens, w_query, w_key, w_value, w_out, encoded, ask, slot)


def shards(tokens, w_query, w_key, w_value, w_out, encoded, nbr_shard, nbr_row):
    shard = nbr_shard.reshape(32)
    row = nbr_row.reshape(32)
    ids = jnp.arange(32, dtype=jnp.int32)
    earlier = (shard[:, None] == shard[None, :]) & (ids[None, :] < ids[:, None])
    slot = shard * 2 + jnp.sum(earlier.astype(jnp.int32), axis=1)
    lane = jnp.arange(128, dtype=jnp.int32)
    want = jnp.where(lane < 2, 2 * jnp.arange(NP, dtype=jnp.int32)[:, None] + lane[None, :], -1)
    ask = jnp.sum(jnp.where(slot[None, None, :] == want[:, :, None], row[None, None, :], 0), axis=2)
    return fused(
        tokens, w_query, w_key, w_value, w_out, encoded, ask.reshape(NP, 1, 128), slot.reshape(1, 32)
    )


def solution(mesh):
    return jax.shard_map(
        shards,
        mesh=mesh,
        in_specs=(
            P(("dp", "mp"), None),
            P(None, "mp"),
            P(None, "mp"),
            P(None, "mp"),
            P("mp", None),
            P("dp", None, None),
            P("dp", None),
            P("dp", None),
        ),
        out_specs=P(("dp", "mp"), None),
        check_vma=False,
    )
```

```python
import math

import jax
import jax.numpy as jnp
from jax import lax
from jax.experimental import pallas as pl
from jax.experimental.pallas import tpu as pltpu
from jax.sharding import PartitionSpec as P

MESH = pl.DeviceIdType.MESH
BF = jnp.bfloat16
F32 = jnp.float32
HD = 128
SPAN = 64
D = 4096
ENC = 896
TOK = 128
NX = 4
NZ = 8
NP = 32
ROWS = 16
E_COLS = ((0, 512), (512, 384))
QZ = 1024
QSPLIT = 288
QU = (D - QZ) // 16
OU = D // 16
SLOTS = ((1, 0), (1, 1), (2, 0), (2, 1), (3, 0), (3, 1), (0, 1))
OUT_CHUNK = 1024


def kernel(
    tok, wq, wk, wv, wo, enc, nbr_v, row_v, nbr_s, o_own, o_in,
    tokv, ttail, wqb, wkb, wvb, wob, band, ask_o, ask_r, rank_v, pick_v, pick_s, send_e, recv_a, recv_b, send_z, encz,
    qb, kb, vb, att, att0, acc, t_own, t_send, r_out, r_in,
    l_sem, sz, rz, sx, rx, es, e1r, e2r, e3r, st, rt,
):
    d = lax.axis_index("dp")
    z = lax.axis_index("mp")
    x = d // 8
    y = lax.rem(d // 2, 4)
    c = lax.rem(d, 2)
    other = (d + 1 - 2 * c, z)
    zdn = (d, lax.rem(z + 7, NZ))
    zup = (d, lax.rem(z + 1, NZ))
    odn = (other[0], zdn[1])
    oup = (other[0], zup[1])

    def plane(px, py):
        return (px * 8 + py * 2 + c, z)

    ring = {
        "x": (plane(lax.rem(x + 1, 4), y), plane(lax.rem(x + 3, 4), y)),
        "y": (plane(x, lax.rem(y + 1, 4)), plane(x, lax.rem(y + 3, 4))),
    }
    cs = pl.ds(pl.multiple_of(c * HD, HD), HD)

    def remote(src, dst, ssem, rsem, dev):
        return pltpu.make_async_remote_copy(
            src_ref=src, dst_ref=dst, send_sem=ssem, recv_sem=rsem, device_id=dev, device_id_type=MESH
        )

    half0 = pl.ds(0, HD)
    local = [
        pltpu.make_async_copy(enc.at[:, pl.ds(pl.multiple_of(z * ROWS, ROWS), ROWS), :], band, l_sem.at[0]),
        pltpu.make_async_copy(tok, tokv.at[pl.ds(0, TOK)], l_sem.at[1]),
        pltpu.make_async_copy(wq.at[:, cs], wqb.at[0, :, half0], l_sem.at[2]),
        pltpu.make_async_copy(wk.at[:, cs], wkb.at[0, :, half0], l_sem.at[3]),
        pltpu.make_async_copy(wv.at[:, cs], wvb.at[0, :, half0], l_sem.at[4]),
        pltpu.make_async_copy(wo.at[cs, :], wob.at[0, half0, :], l_sem.at[5]),
    ]
    for copy in local:
        copy.start()

    bar = pltpu.get_barrier_semaphore()

    def greet_plane(k, carry):
        pl.semaphore_signal(bar, inc=1, device_id=(lax.rem(d + k, NP), z), device_id_type=MESH)
        return carry

    def greet_z(k, carry):
        pl.semaphore_signal(bar, inc=1, device_id=(d, lax.rem(z + k, NZ)), device_id_type=MESH)
        return carry

    lax.fori_loop(1, NP, greet_plane, 0)
    lax.fori_loop(1, NZ, greet_z, 0)
    pl.semaphore_signal(bar, inc=1, device_id=odn, device_id_type=MESH)
    pl.semaphore_signal(bar, inc=1, device_id=oup, device_id_type=MESH)
    pl.semaphore_wait(bar, NP - 1 + NZ - 1 + 2)

    q_slice = (y * 4 + x, x * 4 + y)
    o_slice = (x * 4 + y, y * 4 + x)

    def q_at(sl, start, size):
        if sl is None:
            return wq.at[pl.ds(start, size), cs]
        return wqb.at[sl[0], pl.ds(start, size), pl.ds(sl[1] * HD, HD)]

    def o_at(sl, start, size):
        if sl is None:
            return wo.at[cs, pl.ds(start, size)]
        return wob.at[sl[0], pl.ds(sl[1] * HD, HD), pl.ds(start, size)]

    def kv_at(arg, buf, sl):
        if sl is None:
            return arg.at[:, cs]
        return buf.at[sl[0], :, pl.ds(sl[1] * HD, HD)]

    def drain(sem, units):
        if units <= D:
            ref = wqb.at[0, pl.ds(0, units), pl.ds(0, HD)]
        else:
            ref = wqb.at[pl.ds(0, 2), pl.ds(0, units // 2), pl.ds(0, HD)]
        pltpu.make_async_copy(ref, ref, sem).wait()

    SL, KV, Q0 = 0, 1, 2

    def z_start(k, part):
        for way in (0, 1):
            src_sl = None if k == 1 else (k - 1, way)
            dst_sl = (k, way) if k < 4 else (0, 1)
            pairs = []
            if part == SL and (k < 4 or way == 0):
                start = pl.multiple_of(QZ + q_slice[way] * QU, 16)
                pairs.append((q_at(src_sl, start, QU), q_at(dst_sl, start, QU)))
                start = pl.multiple_of(o_slice[way] * OU, 128)
                pairs.append((o_at(src_sl, start, OU), o_at(dst_sl, start, OU)))
            elif part == KV:
                if k < 4 or way == 0:
                    pairs.append((kv_at(wk, wkb, src_sl), kv_at(wk, wkb, dst_sl)))
                if k < 4 or way == 1:
                    pairs.append((kv_at(wv, wvb, src_sl), kv_at(wv, wvb, dst_sl)))
            elif part == Q0:
                start, size = (0, QZ) if k < 4 else ((0, QSPLIT) if way == 0 else (QSPLIT, QZ - QSPLIT))
                pairs.append((q_at(src_sl, start, size), q_at(dst_sl, start, size)))
            for src, dst in pairs:
                remote(src, dst, sz.at[k - 1, part], rz.at[k - 1, part], zup if way else zdn).start()

    def z_units(k, part):
        units = {SL: QU + OU, KV: 2 * ENC, Q0: QZ}[part]
        return 2 * units if k < 4 else units

    def z_wait(k, part):
        drain(rz.at[k - 1, part], z_units(k, part))

    def view(arr, sl, start, size):
        if arr == 0:
            return q_at(sl, pl.multiple_of(QZ + start, 16), size)
        return o_at(sl, pl.multiple_of(start, 128), size)

    def x_start(t, phase, arr):
        sl = SLOTS[t]
        u = (QU, OU)[arr]
        x_first = (arr == 0) == (t % 2 == 0)
        i1, i2 = (x, y) if x_first else (y, x)
        up, dn = ring["x" if x_first == (phase < 2) else "y"]
        if phase == 0:
            spans = [((i2 * 4 + i1) * u, u)] * 2
        elif phase == 1:
            spans = [
                ((i2 * 4 + lax.rem(i1 + 3, 4)) * u, u // 2),
                ((i2 * 4 + lax.rem(i1 + 1, 4)) * u + u // 2, u // 2),
            ]
        elif phase == 2:
            spans = [(i2 * 4 * u, 4 * u)] * 2
        else:
            spans = [
                (lax.rem(i2 + 3, 4) * 4 * u, 2 * u),
                (lax.rem(i2 + 1, 4) * 4 * u + 2 * u, 2 * u),
            ]
        for way, dev in enumerate((up, dn)):
            ref = view(arr, sl, *spans[way])
            remote(ref, ref, sx.at[t], rx.at[arr, t, phase], dev).start()

    def x_wait(t, phase, arr):
        drain(rx.at[arr, t, phase], 2 * (QU, OU)[arr] * (2, 1, 8, 4)[phase] // 2)

    def ph1(t):
        for arr in (0, 1):
            x_start(t, 0, arr)

    def step(t, phase, only=None):
        for arr in (0, 1) if only is None else (only,):
            x_wait(t, phase, arr)
            if phase < 3:
                x_start(t, phase + 1, arr)

    z_start(1, SL)
    last16 = pl.ds(TOK - 16, 16)
    tail_in = remote(tok.at[last16], ttail, st.at[0], rt.at[0], zup)
    tail_in.start()

    def each(n, f):
        def body(k, carry):
            f(k)
            return carry

        lax.fori_loop(1, n, body, 0)

    def whole(ref, sem):
        return pltpu.make_async_copy(ref, ref, sem)

    ask_o[...] = jnp.full((8, 128), -16, jnp.int32)
    ask_o[0:2, 0:16] = nbr_v[...] * 16 + row_v[...]

    def ask_copy(k):
        p = lax.rem(d + k, NP)
        remote(ask_o, ask_r.at[d], es.at[0], es.at[1], (p, z)).start()

    each(NP, ask_copy)
    ask_r[pl.ds(d, 1)] = ask_o[...][None]
    place = 2 * lax.broadcasted_iota(jnp.int32, (8, 128), 1) + lax.broadcasted_iota(jnp.int32, (8, 128), 0)
    mine = lax.shift_right_arithmetic(ask_o[...], 4)
    for f in range(32):
        same = jnp.logical_and(mine == nbr_s[f % 2, f // 2], place < f)
        rank_v[f] = jnp.where(same, 1, 0)
    rank = jnp.max(jnp.max(rank_v[...], axis=1, keepdims=True), axis=2, keepdims=True)
    pick_v[NP:, :, :] = jnp.broadcast_to(rank, (32, 1, 128))
    local[0].wait()
    whole(ask_r.at[pl.ds(0, NP - 1)], es.at[1]).wait()
    codes = ask_r[...]
    hit = lax.shift_right_arithmetic(codes, 4) == d
    key = place[None] * 16 + jnp.bitwise_and(codes, 15)
    low = jnp.where(hit, key, 1 << 20)
    low = jnp.min(jnp.min(low, axis=1, keepdims=True), axis=2, keepdims=True)
    high = jnp.where(hit, key, 0)
    high = jnp.max(jnp.max(high, axis=1, keepdims=True), axis=2, keepdims=True)
    lane = lax.broadcasted_iota(jnp.int32, (NP, 1, 128), 2)
    pick_v[:NP, :, :] = jnp.bitwise_and(jnp.where(lane == 0, low, high), 15)
    to_smem = pltpu.make_async_copy(pick_v, pick_s, l_sem.at[6])
    to_smem.start()
    to_smem.wait()

    recv_e = (recv_a, recv_b)

    def e1_start(part):
        cols = pl.ds(*E_COLS[part])

        def pick(s, carry):
            for j in range(2):
                send_e[s, j, :, cols] = band[pick_s[s, 0, j], :, cols]
            return carry

        lax.fori_loop(0, NP, pick, 0)

        def copy(k):
            p = lax.rem(d + k, NP)
            remote(
                send_e.at[p, :, :, cols], recv_e[part].at[pl.ds(2 * d, 2)], es.at[2], e1r.at[part], (p, z)
            ).start()

        each(NP, copy)
        recv_e[part][pl.ds(2 * d, 2)] = send_e[d, :, :, cols]

    my_rows = pl.ds(pl.multiple_of(z * ROWS, ROWS), ROWS)

    def e2_start(part):
        cols = pl.ds(*E_COLS[part])
        whole(recv_e[part].at[pl.ds(0, 2 * NP - 2)], e1r.at[part]).wait()

        def pick(mz, carry):
            spans = (lax.rem(2 * mz + 15, 16), 2 * mz)
            for i in range(4):
                span, n = spans[i // 2], i % 2
                place = 2 * nbr_s[n, span] + pick_s[NP + 2 * span + n, 0, 0]
                send_z[mz, i, :, cols] = recv_e[part][place]
            return carry

        lax.fori_loop(0, NZ, pick, 0)

        def copy(k):
            p = lax.rem(z + k, NZ)
            remote(
                send_z.at[p, :, :, cols], encz.at[pl.ds(0, 4), my_rows, cols], es.at[4], e2r.at[part], (d, p)
            ).start()

        each(NZ, copy)
        encz[pl.ds(0, 4), my_rows, cols] = send_z[z, :, :, cols]

    def e3_copy(part):
        cols = pl.ds(*E_COLS[part])
        return remote(encz.at[pl.ds(0, 4), :, cols], encz.at[pl.ds(4, 4), :, cols], es.at[6], e3r.at[part], other)

    def e3_start(part):
        cols = pl.ds(*E_COLS[part])
        whole(send_z.at[pl.ds(0, NZ - 1), :, :, cols], e2r.at[part]).wait()
        e3_copy(part).start()

    for part in range(len(E_COLS)):
        e1_start(part)
    z_wait(1, SL)
    z_start(2, SL)
    ph1(0)
    ph1(1)
    z_start(1, KV)
    z_start(1, Q0)

    local[1].wait()
    tail_in.wait_recv()
    is15 = lax.broadcasted_iota(jnp.int32, (16, D), 0) == 15
    tokv[TOK - 16 : TOK, :] = jnp.where(is15, ttail[...], tokv[TOK - 16 : TOK, :])
    tok_x = remote(tokv.at[pl.ds(0, TOK)], tokv.at[pl.ds(TOK, TOK)], st.at[1], rt.at[1], other)
    tok_x.start()
    z_wait(2, SL)
    z_start(3, SL)
    ph1(2)
    ph1(3)
    z_wait(3, SL)
    z_start(4, SL)
    ph1(4)
    ph1(5)
    z_wait(4, SL)
    ph1(6)

    def project(pair, half):
        lanes = pl.ds(0, 256) if half is None else pl.ds(half * HD, HD)
        width = 256 if half is None else HD

        def body(k, total):
            start = pl.multiple_of(k * 2048, 2048)
            return total + jnp.dot(
                tokv[:, pl.ds(start, 2048)], wqb[pair, pl.ds(start, 2048), lanes], preferred_element_type=F32
            )

        total = lax.fori_loop(0, D // 2048, body, jnp.zeros((2 * TOK, width), F32))
        qb[pair, :, lanes] = total.astype(BF)

    def keys_values(pair, half):
        lanes = pl.ds(0, 256) if half is None else pl.ds(half * HD, HD)

        def body(u, carry):
            rows = encz[pl.ds(4 * u, 4)].reshape(512, ENC)
            keys = jnp.dot(rows, wkb[pair, :, lanes], preferred_element_type=F32)
            kb[pl.ds(2 * u, 2), :, lanes] = keys.astype(BF).reshape(2, 256, -1)
            values = jnp.dot(rows, wvb[pair, :, lanes], preferred_element_type=F32)
            vb[pl.ds(2 * u, 2), :, lanes] = values.astype(BF).reshape(2, 256, -1)
            return carry

        lax.fori_loop(0, 2, body, 0)

    row_id = lax.broadcasted_iota(jnp.int32, (TOK, 256), 0)
    in_b = jnp.logical_and(row_id >= SPAN - 1, row_id < TOK - 1)
    blank = jnp.logical_and(lax.broadcasted_iota(jnp.int32, (TOK, HD), 0) < SPAN - 1, z == 0)

    def attend(pair, half, dst):
        halves = (0, 1) if half is None else (half,)
        for s in range(2):
            for h in halves:
                lanes = pl.ds(h * HD, HD)
                q = qb[pair, s * TOK : (s + 1) * TOK, lanes]
                ka, kb_ = kb[2 * s, :, lanes], kb[2 * s + 1, :, lanes]
                dims = (((1,), (1,)), ((), ()))
                sa_ = lax.dot_general(q, ka, dims, preferred_element_type=F32)
                sb_ = lax.dot_general(q, kb_, dims, preferred_element_type=F32)
                scores = jnp.where(in_b, sb_, sa_) * F32(1.0 / math.sqrt(HD))
                peak = jnp.max(scores, axis=1, keepdims=True)
                e = jnp.exp(scores - peak)
                total = jnp.sum(e, axis=1, keepdims=True)
                wa = jnp.where(in_b, 0.0, e).astype(BF)
                wb = jnp.where(in_b, e, 0.0).astype(BF)
                o = jnp.dot(wa, vb[2 * s, :, lanes], preferred_element_type=F32)
                o = o + jnp.dot(wb, vb[2 * s + 1, :, lanes], preferred_element_type=F32)
                o = jnp.where(blank, 0.0, o / total)
                dst[s * TOK : (s + 1) * TOK, lanes] = o.astype(BF)

    def add_out(pair, is_first):
        def body(k, carry):
            cols = pl.ds(pl.multiple_of(k * OUT_CHUNK, OUT_CHUNK), OUT_CHUNK)
            term = jnp.dot(att[...], wob[pair, :, cols], preferred_element_type=F32)
            acc[:, cols] = term if is_first else acc[:, cols] + term
            return carry

        lax.fori_loop(0, D // OUT_CHUNK, body, 0)

    step(0, 0)
    step(1, 0)
    step(2, 0)
    step(3, 0)
    z_wait(1, KV)
    z_start(2, KV)
    step(4, 0)
    step(5, 0)
    step(6, 0)
    step(0, 1)
    z_wait(1, Q0)
    z_start(2, Q0)
    step(1, 1)
    tok_x.wait_recv()
    local[2].wait()
    project(0, 0)
    step(2, 1)
    e2_start(0)
    e2_start(1)
    z_wait(2, KV)
    z_start(3, KV)
    step(3, 1)
    step(0, 2)
    z_wait(2, Q0)
    z_start(3, Q0)
    step(1, 2)
    step(4, 1)
    step(2, 2)
    step(5, 1)
    step(0, 3)
    step(1, 3)
    project(1, None)
    step(3, 2)
    step(6, 1)
    e3_start(0)
    e3_start(1)
    for part in range(len(E_COLS)):
        e3_copy(part).wait_recv()
    local[3].wait()
    local[4].wait()
    local[5].wait()
    whole(ask_r.at[pl.ds(0, NP - 1)], es.at[0]).wait()
    whole(send_e.at[pl.ds(0, NP - 1)], es.at[2]).wait()
    tail_in.wait_send()
    tok_x.wait_send()
    step(2, 3)
    keys_values(0, 0)
    attend(0, 0, att0)
    z_wait(3, KV)
    z_start(4, KV)
    keys_values(1, None)
    step(4, 2)
    attend(1, None, att)
    add_out(1, True)
    z_wait(3, Q0)
    z_start(4, Q0)
    step(3, 3)
    project(2, None)
    keys_values(2, None)
    step(5, 2)
    attend(2, None, att)
    add_out(2, False)
    step(4, 3)
    step(6, 2)
    step(5, 3)
    project(3, None)
    keys_values(3, None)
    attend(3, None, att)
    add_out(3, False)
    whole(send_z.at[pl.ds(0, NZ - 1)], es.at[4]).wait()
    whole(encz.at[pl.ds(0, 4)], es.at[6]).wait()
    for k in range(1, 4):
        for part in (SL, KV, Q0):
            drain(sz.at[k - 1, part], z_units(k, part))
    for t in range(6):
        drain(sx.at[t], 15 * (QU + OU))
    z_wait(4, KV)
    keys_values(0, 1)
    z_wait(4, Q0)
    step(6, 3)
    project(0, 1)
    attend(0, 1, att0)

    def last(k, carry):
        cols = pl.ds(pl.multiple_of(k * OUT_CHUNK, OUT_CHUNK), OUT_CHUNK)
        term = acc[:, cols] + jnp.dot(att0[...], wob[0, :, cols], preferred_element_type=F32)
        term = term.astype(BF)
        edge15 = lax.broadcasted_iota(jnp.int32, (16, OUT_CHUNK), 0) == 15
        for s, buf in enumerate((t_own, t_send)):
            edge = term[(s + 1) * TOK - 16 : (s + 1) * TOK]
            buf[0 : TOK - 16, cols] = term[s * TOK : (s + 1) * TOK - 16]
            buf[TOK - 16 : TOK, cols] = jnp.where(edge15, jnp.zeros_like(edge), edge)
            r_out[s, :, cols] = edge
        remote(t_send.at[:, cols], o_in.at[:, cols], st.at[3], rt.at[3], other).start()
        remote(r_out.at[0, :, cols], r_in.at[0, :, cols], st.at[4], rt.at[4], zdn).start()
        remote(r_out.at[1, :, cols], r_in.at[1, :, cols], st.at[5], rt.at[5], odn).start()
        top = pl.ds(0, TOK - 16)
        pltpu.make_async_copy(t_own.at[top, cols], o_own.at[top, cols], l_sem.at[7]).start()
        return carry

    lax.fori_loop(0, D // OUT_CHUNK, last, 0)
    for part in (SL, KV, Q0):
        drain(sz.at[3, part], z_units(4, part))
    drain(sx.at[6], 15 * (QU + OU))
    whole(r_in.at[0], rt.at[4]).wait()
    whole(r_in.at[1], rt.at[5]).wait()
    edge = (r_in[0].astype(F32) + r_in[1].astype(F32)).astype(BF)
    t_own[TOK - 16 : TOK, :] = jnp.where(is15, edge, t_own[TOK - 16 : TOK, :])
    bottom = pltpu.make_async_copy(t_own.at[last16], o_own.at[last16], l_sem.at[6])
    bottom.start()
    whole(t_own.at[pl.ds(0, TOK - 16)], l_sem.at[7]).wait()
    whole(r_out.at[0], st.at[4]).wait()
    whole(r_out.at[1], st.at[5]).wait()
    whole(t_send, st.at[3]).wait()
    whole(o_in, rt.at[3]).wait()
    bottom.wait()


def fused(tokens, w_query, w_key, w_value, w_out, encoded, nbr_shard, nbr_row):
    any_ = pl.BlockSpec(memory_space=pl.ANY)
    vmem = pl.BlockSpec(memory_space=pltpu.VMEM)
    smem = pl.BlockSpec(memory_space=pltpu.SMEM)
    dma = pltpu.SemaphoreType.DMA
    V = pltpu.VMEM
    return pl.pallas_call(
        kernel,
        out_shape=(jax.ShapeDtypeStruct((TOK, D), BF), jax.ShapeDtypeStruct((TOK, D), BF)),
        in_specs=[any_] * 6 + [vmem, vmem, smem],
        out_specs=(any_, any_),
        scratch_shapes=[
            V((2 * TOK, D), BF),
            V((16, D), BF),
            V((4, D, 256), BF),
            V((4, ENC, 256), BF),
            V((4, ENC, 256), BF),
            V((4, 256, D), BF),
            V((16, ROWS, ENC), BF),
            V((8, 128), jnp.int32),
            V((NP, 8, 128), jnp.int32),
            V((32, 8, 128), jnp.int32),
            V((2 * NP, 1, 128), jnp.int32),
            pltpu.SMEM((2 * NP, 1, 128), jnp.int32),
            V((NP, 2, ROWS, ENC), BF),
            V((2 * NP, ROWS, E_COLS[0][1]), BF),
            V((2 * NP, ROWS, E_COLS[1][1]), BF),
            V((NZ, 4, ROWS, ENC), BF),
            V((8, 128, ENC), BF),
            V((4, 2 * TOK, 256), BF),
            V((4, 256, 256), BF),
            V((4, 256, 256), BF),
            V((2 * TOK, 256), BF),
            V((2 * TOK, 256), BF),
            V((2 * TOK, D), F32),
            V((TOK, D), BF),
            V((TOK, D), BF),
            V((2, 16, D), BF),
            V((2, 16, D), BF),
            dma((8,)),
            dma((4, 3)),
            dma((4, 3)),
            dma((7,)),
            dma((2, 7, 4)),
            dma((7,)),
            dma((len(E_COLS),)),
            dma((len(E_COLS),)),
            dma((len(E_COLS),)),
            dma((6,)),
            dma((6,)),
        ],
        compiler_params=pltpu.CompilerParams(
            collective_id=0, has_side_effects=True, vmem_limit_bytes=56 * 1024 * 1024
        ),
    )(tokens, w_query, w_key, w_value, w_out, encoded, nbr_shard, nbr_row, nbr_shard)


def shards(tokens, w_query, w_key, w_value, w_out, encoded, nbr_shard, nbr_row):
    own, received = fused(
        tokens, w_query, w_key, w_value, w_out, encoded, nbr_shard.T, nbr_row.T
    )
    return (own.astype(F32) + received.astype(F32)).astype(BF)


def solution(mesh):
    return jax.shard_map(
        shards,
        mesh=mesh,
        in_specs=(
            P(("dp", "mp"), None),
            P(None, "mp"),
            P(None, "mp"),
            P(None, "mp"),
            P("mp", None),
            P("dp", None, None),
            P("dp", None),
            P("dp", None),
        ),
        out_specs=P(("dp", "mp"), None),
        check_vma=False,
    )
```

```python
import math

import jax
import jax.numpy as jnp
from jax import lax
from jax.experimental import pallas as pl
from jax.experimental.pallas import tpu as pltpu
from jax.sharding import PartitionSpec as P

MESH = pl.DeviceIdType.MESH
BF = jnp.bfloat16
F32 = jnp.float32
HD = 128
SPAN = 64
D = 4096
ENC = 896
TOK = 128
NX = 4
NZ = 8
NP = 32
ROWS = 16
E_COLS = ((0, 512), (512, 384))
QZ = 1024
QSPLIT = 288
QU = (D - QZ) // 16
OU = D // 16
SLOTS = ((1, 0), (1, 1), (2, 0), (2, 1), (3, 0), (3, 1), (0, 1))
OUT_CHUNK = 1024


def kernel(
    tok, wq, wk, wv, wo, enc, nbr_v, row_v, nbr_s, o_own, o_in,
    tokv, e_out, e_in, wqb, wkb, wvb, wob, band, ask_o, ask_r, rank_v, pick_v, pick_s, send_e, recv_a, recv_b, send_z, encz,
    qb, kb, vb, att, att0, acc, t_own, t_send, r_out,
    l_sem, sz, rz, sx, rx, es, e1r, e2r, e3r, st, rt,
):
    d = lax.axis_index("dp")
    z = lax.axis_index("mp")
    x = d // 8
    y = lax.rem(d // 2, 4)
    c = lax.rem(d, 2)
    other = (d + 1 - 2 * c, z)
    zdn = (d, lax.rem(z + 7, NZ))
    zup = (d, lax.rem(z + 1, NZ))
    odn = (other[0], zdn[1])
    oup = (other[0], zup[1])

    def plane(px, py):
        return (px * 8 + py * 2 + c, z)

    ring = {
        "x": (plane(lax.rem(x + 1, 4), y), plane(lax.rem(x + 3, 4), y)),
        "y": (plane(x, lax.rem(y + 1, 4)), plane(x, lax.rem(y + 3, 4))),
    }
    cs = pl.ds(pl.multiple_of(c * HD, HD), HD)

    def remote(src, dst, ssem, rsem, dev):
        return pltpu.make_async_remote_copy(
            src_ref=src, dst_ref=dst, send_sem=ssem, recv_sem=rsem, device_id=dev, device_id_type=MESH
        )

    half0 = pl.ds(0, HD)
    local = [
        pltpu.make_async_copy(enc.at[:, pl.ds(pl.multiple_of(z * ROWS, ROWS), ROWS), :], band, l_sem.at[0]),
        pltpu.make_async_copy(tok, tokv.at[pl.ds(0, TOK)], l_sem.at[1]),
        pltpu.make_async_copy(wq.at[:, cs], wqb.at[0, :, half0], l_sem.at[2]),
        pltpu.make_async_copy(wk.at[:, cs], wkb.at[0, :, half0], l_sem.at[3]),
        pltpu.make_async_copy(wv.at[:, cs], wvb.at[0, :, half0], l_sem.at[4]),
        pltpu.make_async_copy(wo.at[cs, :], wob.at[0, half0, :], l_sem.at[5]),
    ]
    for copy in local:
        copy.start()

    bar = pltpu.get_barrier_semaphore()

    def greet_plane(k, carry):
        pl.semaphore_signal(bar, inc=1, device_id=(lax.rem(d + k, NP), z), device_id_type=MESH)
        return carry

    def greet_z(k, carry):
        pl.semaphore_signal(bar, inc=1, device_id=(d, lax.rem(z + k, NZ)), device_id_type=MESH)
        return carry

    lax.fori_loop(1, NP, greet_plane, 0)
    lax.fori_loop(1, NZ, greet_z, 0)
    pl.semaphore_signal(bar, inc=1, device_id=odn, device_id_type=MESH)
    pl.semaphore_signal(bar, inc=1, device_id=oup, device_id_type=MESH)
    pl.semaphore_wait(bar, NP - 1 + NZ - 1 + 2)

    q_slice = (y * 4 + x, x * 4 + y)
    o_slice = (x * 4 + y, y * 4 + x)

    def q_at(sl, start, size):
        if sl is None:
            return wq.at[pl.ds(start, size), cs]
        return wqb.at[sl[0], pl.ds(start, size), pl.ds(sl[1] * HD, HD)]

    def o_at(sl, start, size):
        if sl is None:
            return wo.at[cs, pl.ds(start, size)]
        return wob.at[sl[0], pl.ds(sl[1] * HD, HD), pl.ds(start, size)]

    def kv_at(arg, buf, sl):
        if sl is None:
            return arg.at[:, cs]
        return buf.at[sl[0], :, pl.ds(sl[1] * HD, HD)]

    def drain(sem, units):
        if units <= D:
            ref = wqb.at[0, pl.ds(0, units), pl.ds(0, HD)]
        else:
            ref = wqb.at[pl.ds(0, 2), pl.ds(0, units // 2), pl.ds(0, HD)]
        pltpu.make_async_copy(ref, ref, sem).wait()

    SL, KV, Q0 = 0, 1, 2

    def z_start(k, part):
        for way in (0, 1):
            src_sl = None if k == 1 else (k - 1, way)
            dst_sl = (k, way) if k < 4 else (0, 1)
            pairs = []
            if part == SL and (k < 4 or way == 0):
                start = pl.multiple_of(QZ + q_slice[way] * QU, 16)
                pairs.append((q_at(src_sl, start, QU), q_at(dst_sl, start, QU)))
                start = pl.multiple_of(o_slice[way] * OU, 128)
                pairs.append((o_at(src_sl, start, OU), o_at(dst_sl, start, OU)))
            elif part == KV:
                if k < 4 or way == 0:
                    pairs.append((kv_at(wk, wkb, src_sl), kv_at(wk, wkb, dst_sl)))
                if k < 4 or way == 1:
                    pairs.append((kv_at(wv, wvb, src_sl), kv_at(wv, wvb, dst_sl)))
            elif part == Q0:
                start, size = (0, QZ) if k < 4 else ((0, QSPLIT) if way == 0 else (QSPLIT, QZ - QSPLIT))
                pairs.append((q_at(src_sl, start, size), q_at(dst_sl, start, size)))
            for src, dst in pairs:
                remote(src, dst, sz.at[k - 1, part], rz.at[k - 1, part], zup if way else zdn).start()

    def z_units(k, part):
        units = {SL: QU + OU, KV: 2 * ENC, Q0: QZ}[part]
        return 2 * units if k < 4 else units

    def z_wait(k, part):
        drain(rz.at[k - 1, part], z_units(k, part))

    def view(arr, sl, start, size):
        if arr == 0:
            return q_at(sl, pl.multiple_of(QZ + start, 16), size)
        return o_at(sl, pl.multiple_of(start, 128), size)

    def x_start(t, phase, arr):
        sl = SLOTS[t]
        u = (QU, OU)[arr]
        x_first = (arr == 0) == (t % 2 == 0)
        i1, i2 = (x, y) if x_first else (y, x)
        up, dn = ring["x" if x_first == (phase < 2) else "y"]
        if phase == 0:
            spans = [((i2 * 4 + i1) * u, u)] * 2
        elif phase == 1:
            spans = [
                ((i2 * 4 + lax.rem(i1 + 3, 4)) * u, u // 2),
                ((i2 * 4 + lax.rem(i1 + 1, 4)) * u + u // 2, u // 2),
            ]
        elif phase == 2:
            spans = [(i2 * 4 * u, 4 * u)] * 2
        else:
            spans = [
                (lax.rem(i2 + 3, 4) * 4 * u, 2 * u),
                (lax.rem(i2 + 1, 4) * 4 * u + 2 * u, 2 * u),
            ]
        for way, dev in enumerate((up, dn)):
            ref = view(arr, sl, *spans[way])
            remote(ref, ref, sx.at[t], rx.at[arr, t, phase], dev).start()

    def x_wait(t, phase, arr):
        drain(rx.at[arr, t, phase], 2 * (QU, OU)[arr] * (2, 1, 8, 4)[phase] // 2)

    def ph1(t):
        for arr in (0, 1):
            x_start(t, 0, arr)

    def step(t, phase, only=None):
        for arr in (0, 1) if only is None else (only,):
            x_wait(t, phase, arr)
            if phase < 3:
                x_start(t, phase + 1, arr)

    z_start(1, SL)
    last16 = pl.ds(TOK - 16, 16)
    is15 = lax.broadcasted_iota(jnp.int32, (16, 256), 0) == 15

    def fold(rows, i):
        row = rows.astype(F32)[15:16, :]
        packed = jnp.zeros((16, 256), F32)
        for j in range(16):
            piece = jnp.broadcast_to(row[:, 256 * j : 256 * (j + 1)], (16, 256))
            packed = jnp.where(lax.broadcasted_iota(jnp.int32, (16, 256), 0) == j, piece, packed)
        e_out[i] = packed.astype(BF)

    def unfold(packed, buf):
        for j in range(16):
            cols = pl.ds(256 * j, 256)
            piece = jnp.broadcast_to(packed[j : j + 1, :], (16, 256))
            buf[TOK - 16 : TOK, cols] = jnp.where(is15, piece, buf[TOK - 16 : TOK, cols].astype(F32)).astype(BF)

    def each(n, f):
        def body(k, carry):
            f(k)
            return carry

        lax.fori_loop(1, n, body, 0)

    def whole(ref, sem):
        return pltpu.make_async_copy(ref, ref, sem)

    ask_o[...] = jnp.full((8, 128), -16, jnp.int32)
    ask_o[0:2, 0:16] = nbr_v[...] * 16 + row_v[...]

    def ask_copy(k):
        p = lax.rem(d + k, NP)
        remote(ask_o, ask_r.at[d], es.at[0], es.at[1], (p, z)).start()

    each(NP, ask_copy)
    z_start(1, KV)
    z_start(1, Q0)
    local[1].wait()
    fold(tokv[TOK - 16 : TOK, :], 0)
    tail_in = remote(e_out.at[0], e_in.at[0], st.at[0], rt.at[0], zup)
    tail_in.start()
    ask_r[pl.ds(d, 1)] = ask_o[...][None]
    place = 2 * lax.broadcasted_iota(jnp.int32, (8, 128), 1) + lax.broadcasted_iota(jnp.int32, (8, 128), 0)
    mine = lax.shift_right_arithmetic(ask_o[...], 4)
    for f in range(32):
        same = jnp.logical_and(mine == nbr_s[f % 2, f // 2], place < f)
        rank_v[f] = jnp.where(same, 1, 0)
    rank = jnp.max(jnp.max(rank_v[...], axis=1, keepdims=True), axis=2, keepdims=True)
    pick_v[NP:, :, :] = jnp.broadcast_to(rank, (32, 1, 128))
    z_wait(1, SL)
    z_start(2, SL)
    ph1(0)
    ph1(1)
    local[0].wait()
    whole(ask_r.at[pl.ds(0, NP - 1)], es.at[1]).wait()
    codes = ask_r[...]
    hit = lax.shift_right_arithmetic(codes, 4) == d
    key = place[None] * 16 + jnp.bitwise_and(codes, 15)
    low = jnp.where(hit, key, 1 << 20)
    low = jnp.min(jnp.min(low, axis=1, keepdims=True), axis=2, keepdims=True)
    high = jnp.where(hit, key, 0)
    high = jnp.max(jnp.max(high, axis=1, keepdims=True), axis=2, keepdims=True)
    lane = lax.broadcasted_iota(jnp.int32, (NP, 1, 128), 2)
    pick_v[:NP, :, :] = jnp.bitwise_and(jnp.where(lane == 0, low, high), 15)
    to_smem = pltpu.make_async_copy(pick_v, pick_s, l_sem.at[6])
    to_smem.start()
    to_smem.wait()

    recv_e = (recv_a, recv_b)

    def e1_start(part):
        cols = pl.ds(*E_COLS[part])

        def pick(s, carry):
            for j in range(2):
                send_e[s, j, :, cols] = band[pick_s[s, 0, j], :, cols]
            return carry

        lax.fori_loop(0, NP, pick, 0)

        def copy(k):
            p = lax.rem(d + k, NP)
            remote(
                send_e.at[p, :, :, cols], recv_e[part].at[pl.ds(2 * d, 2)], es.at[2], e1r.at[part], (p, z)
            ).start()

        each(NP, copy)
        recv_e[part][pl.ds(2 * d, 2)] = send_e[d, :, :, cols]

    my_rows = pl.ds(pl.multiple_of(z * ROWS, ROWS), ROWS)

    def e2_start(part):
        cols = pl.ds(*E_COLS[part])
        whole(recv_e[part].at[pl.ds(0, 2 * NP - 2)], e1r.at[part]).wait()

        def pick(mz, carry):
            spans = (lax.rem(2 * mz + 15, 16), 2 * mz)
            for i in range(4):
                span, n = spans[i // 2], i % 2
                place = 2 * nbr_s[n, span] + pick_s[NP + 2 * span + n, 0, 0]
                send_z[mz, i, :, cols] = recv_e[part][place]
            return carry

        lax.fori_loop(0, NZ, pick, 0)

        def copy(k):
            p = lax.rem(z + k, NZ)
            remote(
                send_z.at[p, :, :, cols], encz.at[pl.ds(0, 4), my_rows, cols], es.at[4], e2r.at[part], (d, p)
            ).start()

        each(NZ, copy)
        encz[pl.ds(0, 4), my_rows, cols] = send_z[z, :, :, cols]

    def e3_copy(part):
        cols = pl.ds(*E_COLS[part])
        return remote(encz.at[pl.ds(0, 4), :, cols], encz.at[pl.ds(4, 4), :, cols], es.at[6], e3r.at[part], other)

    def e3_start(part):
        cols = pl.ds(*E_COLS[part])
        whole(send_z.at[pl.ds(0, NZ - 1), :, :, cols], e2r.at[part]).wait()
        e3_copy(part).start()

    for part in range(len(E_COLS)):
        e1_start(part)

    tail_in.wait_recv()
    unfold(e_in[0].astype(F32), tokv)
    tok_x = remote(tokv.at[pl.ds(0, TOK)], tokv.at[pl.ds(TOK, TOK)], st.at[1], rt.at[1], other)
    tok_x.start()
    z_wait(2, SL)
    z_start(3, SL)
    ph1(2)
    ph1(3)
    z_wait(3, SL)
    z_start(4, SL)
    ph1(4)
    ph1(5)
    z_wait(4, SL)
    ph1(6)

    def project(pair, half):
        lanes = pl.ds(0, 256) if half is None else pl.ds(half * HD, HD)
        width = 256 if half is None else HD

        def body(k, total):
            start = pl.multiple_of(k * 2048, 2048)
            return total + jnp.dot(
                tokv[:, pl.ds(start, 2048)], wqb[pair, pl.ds(start, 2048), lanes], preferred_element_type=F32
            )

        total = lax.fori_loop(0, D // 2048, body, jnp.zeros((2 * TOK, width), F32))
        qb[pair, :, lanes] = total.astype(BF)

    def keys_values(pair, half):
        lanes = pl.ds(0, 256) if half is None else pl.ds(half * HD, HD)

        def body(u, carry):
            rows = encz[pl.ds(4 * u, 4)].reshape(512, ENC)
            keys = jnp.dot(rows, wkb[pair, :, lanes], preferred_element_type=F32)
            kb[pl.ds(2 * u, 2), :, lanes] = keys.astype(BF).reshape(2, 256, -1)
            values = jnp.dot(rows, wvb[pair, :, lanes], preferred_element_type=F32)
            vb[pl.ds(2 * u, 2), :, lanes] = values.astype(BF).reshape(2, 256, -1)
            return carry

        lax.fori_loop(0, 2, body, 0)

    row_id = lax.broadcasted_iota(jnp.int32, (TOK, 256), 0)
    in_b = jnp.logical_and(row_id >= SPAN - 1, row_id < TOK - 1)
    blank = jnp.logical_and(lax.broadcasted_iota(jnp.int32, (TOK, HD), 0) < SPAN - 1, z == 0)

    def attend(pair, half, dst):
        halves = (0, 1) if half is None else (half,)
        for s in range(2):
            for h in halves:
                lanes = pl.ds(h * HD, HD)
                q = qb[pair, s * TOK : (s + 1) * TOK, lanes]
                ka, kb_ = kb[2 * s, :, lanes], kb[2 * s + 1, :, lanes]
                dims = (((1,), (1,)), ((), ()))
                sa_ = lax.dot_general(q, ka, dims, preferred_element_type=F32)
                sb_ = lax.dot_general(q, kb_, dims, preferred_element_type=F32)
                scores = jnp.where(in_b, sb_, sa_) * F32(1.0 / math.sqrt(HD))
                peak = jnp.max(scores, axis=1, keepdims=True)
                e = jnp.exp(scores - peak)
                total = jnp.sum(e, axis=1, keepdims=True)
                wa = jnp.where(in_b, 0.0, e).astype(BF)
                wb = jnp.where(in_b, e, 0.0).astype(BF)
                o = jnp.dot(wa, vb[2 * s, :, lanes], preferred_element_type=F32)
                o = o + jnp.dot(wb, vb[2 * s + 1, :, lanes], preferred_element_type=F32)
                o = jnp.where(blank, 0.0, o / total)
                dst[s * TOK : (s + 1) * TOK, lanes] = o.astype(BF)

    def add_out(pair, is_first):
        def body(k, carry):
            cols = pl.ds(pl.multiple_of(k * OUT_CHUNK, OUT_CHUNK), OUT_CHUNK)
            term = jnp.dot(att[...], wob[pair, :, cols], preferred_element_type=F32)
            acc[:, cols] = term if is_first else acc[:, cols] + term
            return carry

        lax.fori_loop(0, D // OUT_CHUNK, body, 0)

    step(0, 0)
    step(1, 0)
    step(2, 0)
    step(3, 0)
    z_wait(1, KV)
    z_start(2, KV)
    step(4, 0)
    step(5, 0)
    step(6, 0)
    step(0, 1)
    z_wait(1, Q0)
    z_start(2, Q0)
    step(1, 1)
    tok_x.wait_recv()
    local[2].wait()
    project(0, 0)
    step(2, 1)
    e2_start(0)
    e2_start(1)
    z_wait(2, KV)
    z_start(3, KV)
    step(3, 1)
    z_wait(2, Q0)
    z_start(3, Q0)
    step(0, 2)
    step(1, 2)
    step(4, 1)
    step(2, 2)
    step(5, 1)
    step(0, 3)
    step(1, 3)
    project(1, None)
    step(3, 2)
    step(6, 1)
    e3_start(0)
    e3_start(1)
    for part in range(len(E_COLS)):
        e3_copy(part).wait_recv()
    local[3].wait()
    local[4].wait()
    local[5].wait()
    whole(ask_r.at[pl.ds(0, NP - 1)], es.at[0]).wait()
    whole(send_e.at[pl.ds(0, NP - 1)], es.at[2]).wait()
    tail_in.wait_send()
    tok_x.wait_send()
    step(2, 3)
    z_wait(3, KV)
    z_start(4, KV)
    keys_values(0, 0)
    attend(0, 0, att0)
    keys_values(1, None)
    step(4, 2)
    attend(1, None, att)
    add_out(1, True)
    z_wait(3, Q0)
    z_start(4, Q0)
    step(3, 3)
    project(2, None)
    keys_values(2, None)
    step(5, 2, 0)
    step(6, 2, 0)
    step(5, 2, 1)
    attend(2, None, att)
    add_out(2, False)
    step(4, 3)
    step(6, 2, 1)
    step(5, 3, 0)
    project(3, None)
    keys_values(3, None)
    attend(3, None, att)
    step(6, 3, 0)
    z_wait(4, KV)
    z_wait(4, Q0)
    keys_values(0, 1)
    project(0, 1)
    attend(0, 1, att0)
    whole(send_z.at[pl.ds(0, NZ - 1)], es.at[4]).wait()
    whole(encz.at[pl.ds(0, 4)], es.at[6]).wait()
    for k in range(1, 4):
        for part in (SL, KV, Q0):
            drain(sz.at[k - 1, part], z_units(k, part))
    for t in range(6):
        drain(sx.at[t], 15 * (QU + OU))
    step(5, 3, 1)
    step(6, 3, 1)

    def last(k, carry):
        cols = pl.ds(pl.multiple_of(k * OUT_CHUNK, OUT_CHUNK), OUT_CHUNK)
        term = acc[:, cols] + jnp.dot(att[...], wob[3, :, cols], preferred_element_type=F32)
        term = term + jnp.dot(att0[...], wob[0, :, cols], preferred_element_type=F32)
        term = term.astype(BF)
        edge15 = lax.broadcasted_iota(jnp.int32, (16, OUT_CHUNK), 0) == 15
        for s, buf in enumerate((t_own, t_send)):
            edge = term[(s + 1) * TOK - 16 : (s + 1) * TOK]
            buf[0 : TOK - 16, cols] = term[s * TOK : (s + 1) * TOK - 16]
            buf[TOK - 16 : TOK, cols] = jnp.where(edge15, jnp.zeros_like(edge), edge)
            r_out[s, :, cols] = edge
        remote(t_send.at[:, cols], o_in.at[:, cols], st.at[3], rt.at[3], other).start()
        top = pl.ds(0, TOK - 16)
        pltpu.make_async_copy(t_own.at[top, cols], o_own.at[top, cols], l_sem.at[7]).start()
        return carry

    lax.fori_loop(0, D // OUT_CHUNK, last, 0)
    edges = []
    for i, dev in ((1, zdn), (2, odn)):
        fold(r_out[i - 1], i)
        edges.append(remote(e_out.at[i], e_in.at[i], st.at[i + 3], rt.at[i + 3], dev))
        edges[-1].start()
    for part in (SL, KV, Q0):
        drain(sz.at[3, part], z_units(4, part))
    drain(sx.at[6], 15 * (QU + OU))
    for edge in edges:
        edge.wait_recv()
    unfold(e_in[1].astype(F32) + e_in[2].astype(F32), t_own)
    bottom = pltpu.make_async_copy(t_own.at[last16], o_own.at[last16], l_sem.at[6])
    bottom.start()
    whole(t_own.at[pl.ds(0, TOK - 16)], l_sem.at[7]).wait()
    for edge in edges:
        edge.wait_send()
    whole(t_send, st.at[3]).wait()
    whole(o_in, rt.at[3]).wait()
    bottom.wait()


def fused(tokens, w_query, w_key, w_value, w_out, encoded, nbr_shard, nbr_row):
    any_ = pl.BlockSpec(memory_space=pl.ANY)
    vmem = pl.BlockSpec(memory_space=pltpu.VMEM)
    smem = pl.BlockSpec(memory_space=pltpu.SMEM)
    dma = pltpu.SemaphoreType.DMA
    V = pltpu.VMEM
    return pl.pallas_call(
        kernel,
        out_shape=(jax.ShapeDtypeStruct((TOK, D), BF), jax.ShapeDtypeStruct((TOK, D), BF)),
        in_specs=[any_] * 6 + [vmem, vmem, smem],
        out_specs=(any_, any_),
        scratch_shapes=[
            V((2 * TOK, D), BF),
            V((3, 16, 256), BF),
            V((3, 16, 256), BF),
            V((4, D, 256), BF),
            V((4, ENC, 256), BF),
            V((4, ENC, 256), BF),
            V((4, 256, D), BF),
            V((16, ROWS, ENC), BF),
            V((8, 128), jnp.int32),
            V((NP, 8, 128), jnp.int32),
            V((32, 8, 128), jnp.int32),
            V((2 * NP, 1, 128), jnp.int32),
            pltpu.SMEM((2 * NP, 1, 128), jnp.int32),
            V((NP, 2, ROWS, ENC), BF),
            V((2 * NP, ROWS, E_COLS[0][1]), BF),
            V((2 * NP, ROWS, E_COLS[1][1]), BF),
            V((NZ, 4, ROWS, ENC), BF),
            V((8, 128, ENC), BF),
            V((4, 2 * TOK, 256), BF),
            V((4, 256, 256), BF),
            V((4, 256, 256), BF),
            V((2 * TOK, 256), BF),
            V((2 * TOK, 256), BF),
            V((2 * TOK, D), F32),
            V((TOK, D), BF),
            V((TOK, D), BF),
            V((2, 16, D), BF),
            dma((8,)),
            dma((4, 3)),
            dma((4, 3)),
            dma((7,)),
            dma((2, 7, 4)),
            dma((7,)),
            dma((len(E_COLS),)),
            dma((len(E_COLS),)),
            dma((len(E_COLS),)),
            dma((6,)),
            dma((6,)),
        ],
        compiler_params=pltpu.CompilerParams(
            collective_id=0, has_side_effects=True, vmem_limit_bytes=56 * 1024 * 1024
        ),
    )(tokens, w_query, w_key, w_value, w_out, encoded, nbr_shard, nbr_row, nbr_shard)


def shards(tokens, w_query, w_key, w_value, w_out, encoded, nbr_shard, nbr_row):
    own, received = fused(
        tokens, w_query, w_key, w_value, w_out, encoded, nbr_shard.T, nbr_row.T
    )
    return (own.astype(F32) + received.astype(F32)).astype(BF)


def solution(mesh):
    return jax.shard_map(
        shards,
        mesh=mesh,
        in_specs=(
            P(("dp", "mp"), None),
            P(None, "mp"),
            P(None, "mp"),
            P(None, "mp"),
            P("mp", None),
            P("dp", None, None),
            P("dp", None),
            P("dp", None),
        ),
        out_specs=P(("dp", "mp"), None),
        check_vma=False,
    )
```

```python
import math

import jax
import jax.numpy as jnp
from jax import lax
from jax.experimental import pallas as pl
from jax.experimental.pallas import tpu as pltpu
from jax.sharding import PartitionSpec as P

MESH = pl.DeviceIdType.MESH
BF = jnp.bfloat16
F32 = jnp.float32
HD = 128
SPAN = 64
D = 4096
ENC = 896
TOK = 128
NX = 4
NZ = 8
NP = 32
ROWS = 16
E_COLS = ((0, 384), (384, 256), (640, 256))
QZ = 1024
QSPLIT = 288
QU = (D - QZ) // 16
OU = D // 16
SLOTS = ((1, 0), (1, 1), (2, 0), (2, 1), (3, 0), (3, 1), (0, 1))
OUT_CHUNK = 1024


def kernel(
    tok, wq, wk, wv, wo, enc, nbr_v, row_v, nbr_s, o_own, o_in,
    tokv, e_out, e_in, wqb, wkb, wvb, wob, band, ask_o, ask_r, rank_v, pick_v, pick_s, send_e, recv_a, recv_b, recv_c, send_z, encz,
    qb, kb, vb, att, att0, acc, t_own, t_send, r_out,
    l_sem, sz, rz, sx, rx, es, e1r, e2r, e3r, st, rt,
):
    d = lax.axis_index("dp")
    z = lax.axis_index("mp")
    x = d // 8
    y = lax.rem(d // 2, 4)
    c = lax.rem(d, 2)
    other = (d + 1 - 2 * c, z)
    zdn = (d, lax.rem(z + 7, NZ))
    zup = (d, lax.rem(z + 1, NZ))
    odn = (other[0], zdn[1])
    oup = (other[0], zup[1])

    def plane(px, py):
        return (px * 8 + py * 2 + c, z)

    ring = {
        "x": (plane(lax.rem(x + 1, 4), y), plane(lax.rem(x + 3, 4), y)),
        "y": (plane(x, lax.rem(y + 1, 4)), plane(x, lax.rem(y + 3, 4))),
    }
    cs = pl.ds(pl.multiple_of(c * HD, HD), HD)

    def remote(src, dst, ssem, rsem, dev):
        return pltpu.make_async_remote_copy(
            src_ref=src, dst_ref=dst, send_sem=ssem, recv_sem=rsem, device_id=dev, device_id_type=MESH
        )

    half0 = pl.ds(0, HD)
    local = [
        pltpu.make_async_copy(enc.at[:, pl.ds(pl.multiple_of(z * ROWS, ROWS), ROWS), :], band, l_sem.at[0]),
        pltpu.make_async_copy(tok, tokv.at[pl.ds(0, TOK)], l_sem.at[1]),
        pltpu.make_async_copy(wq.at[:, cs], wqb.at[0, :, half0], l_sem.at[2]),
        pltpu.make_async_copy(wk.at[:, cs], wkb.at[0, :, half0], l_sem.at[3]),
        pltpu.make_async_copy(wv.at[:, cs], wvb.at[0, :, half0], l_sem.at[4]),
        pltpu.make_async_copy(wo.at[cs, :], wob.at[0, half0, :], l_sem.at[5]),
    ]
    for copy in local:
        copy.start()

    bar = pltpu.get_barrier_semaphore()

    def greet_plane(k, carry):
        pl.semaphore_signal(bar, inc=1, device_id=(lax.rem(d + k, NP), z), device_id_type=MESH)
        return carry

    def greet_z(k, carry):
        pl.semaphore_signal(bar, inc=1, device_id=(d, lax.rem(z + k, NZ)), device_id_type=MESH)
        return carry

    lax.fori_loop(1, NP, greet_plane, 0)
    lax.fori_loop(1, NZ, greet_z, 0)
    pl.semaphore_signal(bar, inc=1, device_id=odn, device_id_type=MESH)
    pl.semaphore_signal(bar, inc=1, device_id=oup, device_id_type=MESH)
    pl.semaphore_wait(bar, NP - 1 + NZ - 1 + 2)

    q_slice = (y * 4 + x, x * 4 + y)
    o_slice = (x * 4 + y, y * 4 + x)

    def q_at(sl, start, size):
        if sl is None:
            return wq.at[pl.ds(start, size), cs]
        return wqb.at[sl[0], pl.ds(start, size), pl.ds(sl[1] * HD, HD)]

    def o_at(sl, start, size):
        if sl is None:
            return wo.at[cs, pl.ds(start, size)]
        return wob.at[sl[0], pl.ds(sl[1] * HD, HD), pl.ds(start, size)]

    def kv_at(arg, buf, sl):
        if sl is None:
            return arg.at[:, cs]
        return buf.at[sl[0], :, pl.ds(sl[1] * HD, HD)]

    def drain(sem, units):
        if units <= D:
            ref = wqb.at[0, pl.ds(0, units), pl.ds(0, HD)]
        else:
            ref = wqb.at[pl.ds(0, 2), pl.ds(0, units // 2), pl.ds(0, HD)]
        pltpu.make_async_copy(ref, ref, sem).wait()

    SL, KV, Q0 = 0, 1, 2

    def z_start(k, part):
        for way in (0, 1):
            src_sl = None if k == 1 else (k - 1, way)
            dst_sl = (k, way) if k < 4 else (0, 1)
            pairs = []
            if part == SL and (k < 4 or way == 0):
                start = pl.multiple_of(QZ + q_slice[way] * QU, 16)
                pairs.append((q_at(src_sl, start, QU), q_at(dst_sl, start, QU)))
                start = pl.multiple_of(o_slice[way] * OU, 128)
                pairs.append((o_at(src_sl, start, OU), o_at(dst_sl, start, OU)))
            elif part == KV:
                if k < 4 or way == 0:
                    pairs.append((kv_at(wk, wkb, src_sl), kv_at(wk, wkb, dst_sl)))
                if k < 4 or way == 1:
                    pairs.append((kv_at(wv, wvb, src_sl), kv_at(wv, wvb, dst_sl)))
            elif part == Q0:
                start, size = (0, QZ) if k < 4 else ((0, QSPLIT) if way == 0 else (QSPLIT, QZ - QSPLIT))
                pairs.append((q_at(src_sl, start, size), q_at(dst_sl, start, size)))
            for src, dst in pairs:
                remote(src, dst, sz.at[k - 1, part], rz.at[k - 1, part], zup if way else zdn).start()

    def z_units(k, part):
        units = {SL: QU + OU, KV: 2 * ENC, Q0: QZ}[part]
        return 2 * units if k < 4 else units

    def z_wait(k, part):
        drain(rz.at[k - 1, part], z_units(k, part))

    def view(arr, sl, start, size):
        if arr == 0:
            return q_at(sl, pl.multiple_of(QZ + start, 16), size)
        return o_at(sl, pl.multiple_of(start, 128), size)

    def x_start(t, phase, arr):
        sl = SLOTS[t]
        u = (QU, OU)[arr]
        x_first = (arr == 0) == (t % 2 == 0)
        i1, i2 = (x, y) if x_first else (y, x)
        up, dn = ring["x" if x_first == (phase < 2) else "y"]
        if phase == 0:
            spans = [((i2 * 4 + i1) * u, u)] * 2
        elif phase == 1:
            spans = [
                ((i2 * 4 + lax.rem(i1 + 3, 4)) * u, u // 2),
                ((i2 * 4 + lax.rem(i1 + 1, 4)) * u + u // 2, u // 2),
            ]
        elif phase == 2:
            spans = [(i2 * 4 * u, 4 * u)] * 2
        else:
            spans = [
                (lax.rem(i2 + 3, 4) * 4 * u, 2 * u),
                (lax.rem(i2 + 1, 4) * 4 * u + 2 * u, 2 * u),
            ]
        for way, dev in enumerate((up, dn)):
            ref = view(arr, sl, *spans[way])
            remote(ref, ref, sx.at[t], rx.at[arr, t, phase], dev).start()

    def x_wait(t, phase, arr):
        drain(rx.at[arr, t, phase], 2 * (QU, OU)[arr] * (2, 1, 8, 4)[phase] // 2)

    def ph1(t):
        for arr in (0, 1):
            x_start(t, 0, arr)

    def step(t, phase, only=None):
        for arr in (0, 1) if only is None else (only,):
            x_wait(t, phase, arr)
            if phase < 3:
                x_start(t, phase + 1, arr)

    z_start(1, SL)
    last16 = pl.ds(TOK - 16, 16)
    is15 = lax.broadcasted_iota(jnp.int32, (16, 256), 0) == 15

    def fold(rows, i):
        row = rows.astype(F32)[15:16, :]
        packed = jnp.zeros((16, 256), F32)
        for j in range(16):
            piece = jnp.broadcast_to(row[:, 256 * j : 256 * (j + 1)], (16, 256))
            packed = jnp.where(lax.broadcasted_iota(jnp.int32, (16, 256), 0) == j, piece, packed)
        e_out[i] = packed.astype(BF)

    def unfold(packed, buf):
        for j in range(16):
            cols = pl.ds(256 * j, 256)
            piece = jnp.broadcast_to(packed[j : j + 1, :], (16, 256))
            buf[TOK - 16 : TOK, cols] = jnp.where(is15, piece, buf[TOK - 16 : TOK, cols].astype(F32)).astype(BF)

    def each(n, f):
        def body(k, carry):
            f(k)
            return carry

        lax.fori_loop(1, n, body, 0)

    def whole(ref, sem):
        return pltpu.make_async_copy(ref, ref, sem)

    ask_o[...] = jnp.full((8, 128), -16, jnp.int32)
    ask_o[0:2, 0:16] = nbr_v[...] * 16 + row_v[...]

    def ask_copy(k):
        p = lax.rem(d + k, NP)
        remote(ask_o, ask_r.at[d], es.at[0], es.at[1], (p, z)).start()

    each(NP, ask_copy)
    z_start(1, KV)
    z_start(1, Q0)
    local[1].wait()
    fold(tokv[TOK - 16 : TOK, :], 0)
    tail_in = remote(e_out.at[0], e_in.at[0], st.at[0], rt.at[0], zup)
    tail_in.start()
    ask_r[pl.ds(d, 1)] = ask_o[...][None]
    place = 2 * lax.broadcasted_iota(jnp.int32, (8, 128), 1) + lax.broadcasted_iota(jnp.int32, (8, 128), 0)
    mine = lax.shift_right_arithmetic(ask_o[...], 4)
    for f in range(32):
        same = jnp.logical_and(mine == nbr_s[f % 2, f // 2], place < f)
        rank_v[f] = jnp.where(same, 1, 0)
    rank = jnp.max(jnp.max(rank_v[...], axis=1, keepdims=True), axis=2, keepdims=True)
    pick_v[NP:, :, :] = jnp.broadcast_to(rank, (32, 1, 128))
    z_wait(1, SL)
    z_start(2, SL)
    ph1(0)
    ph1(1)
    local[0].wait()
    whole(ask_r.at[pl.ds(0, NP - 1)], es.at[1]).wait()
    codes = ask_r[...]
    hit = lax.shift_right_arithmetic(codes, 4) == d
    key = place[None] * 16 + jnp.bitwise_and(codes, 15)
    low = jnp.where(hit, key, 1 << 20)
    low = jnp.min(jnp.min(low, axis=1, keepdims=True), axis=2, keepdims=True)
    high = jnp.where(hit, key, 0)
    high = jnp.max(jnp.max(high, axis=1, keepdims=True), axis=2, keepdims=True)
    lane = lax.broadcasted_iota(jnp.int32, (NP, 1, 128), 2)
    pick_v[:NP, :, :] = jnp.bitwise_and(jnp.where(lane == 0, low, high), 15)
    to_smem = pltpu.make_async_copy(pick_v, pick_s, l_sem.at[6])
    to_smem.start()
    to_smem.wait()

    recv_e = (recv_a, recv_b, recv_c)

    def e1_start(part):
        cols = pl.ds(*E_COLS[part])

        def pick(s, carry):
            for j in range(2):
                send_e[s, j, :, cols] = band[pick_s[s, 0, j], :, cols]
            return carry

        lax.fori_loop(0, NP, pick, 0)

        def copy(k):
            p = lax.rem(d + k, NP)
            remote(
                send_e.at[p, :, :, cols], recv_e[part].at[pl.ds(2 * d, 2)], es.at[2], e1r.at[part], (p, z)
            ).start()

        each(NP, copy)
        recv_e[part][pl.ds(2 * d, 2)] = send_e[d, :, :, cols]

    my_rows = pl.ds(pl.multiple_of(z * ROWS, ROWS), ROWS)

    def e2_start(part):
        cols = pl.ds(*E_COLS[part])
        whole(recv_e[part].at[pl.ds(0, 2 * NP - 2)], e1r.at[part]).wait()

        def pick(mz, carry):
            spans = (lax.rem(2 * mz + 15, 16), 2 * mz)
            for i in range(4):
                span, n = spans[i // 2], i % 2
                place = 2 * nbr_s[n, span] + pick_s[NP + 2 * span + n, 0, 0]
                send_z[mz, i, :, cols] = recv_e[part][place]
            return carry

        lax.fori_loop(0, NZ, pick, 0)

        def copy(k):
            p = lax.rem(z + k, NZ)
            remote(
                send_z.at[p, :, :, cols], encz.at[pl.ds(0, 4), my_rows, cols], es.at[4], e2r.at[part], (d, p)
            ).start()

        each(NZ, copy)
        encz[pl.ds(0, 4), my_rows, cols] = send_z[z, :, :, cols]

    def e3_copy(part):
        cols = pl.ds(*E_COLS[part])
        return remote(encz.at[pl.ds(0, 4), :, cols], encz.at[pl.ds(4, 4), :, cols], es.at[6], e3r.at[part], other)

    def e3_start(part):
        cols = pl.ds(*E_COLS[part])
        whole(send_z.at[pl.ds(0, NZ - 1), :, :, cols], e2r.at[part]).wait()
        e3_copy(part).start()

    for part in range(len(E_COLS)):
        e1_start(part)

    tail_in.wait_recv()
    unfold(e_in[0].astype(F32), tokv)
    tok_x = remote(tokv.at[pl.ds(0, TOK)], tokv.at[pl.ds(TOK, TOK)], st.at[1], rt.at[1], other)
    tok_x.start()
    z_wait(2, SL)
    z_start(3, SL)
    ph1(2)
    ph1(3)
    z_wait(3, SL)
    z_start(4, SL)
    ph1(4)
    ph1(5)
    z_wait(4, SL)
    ph1(6)

    def project(pair, half):
        lanes = pl.ds(0, 256) if half is None else pl.ds(half * HD, HD)
        width = 256 if half is None else HD

        def body(k, total):
            start = pl.multiple_of(k * 2048, 2048)
            return total + jnp.dot(
                tokv[:, pl.ds(start, 2048)], wqb[pair, pl.ds(start, 2048), lanes], preferred_element_type=F32
            )

        total = lax.fori_loop(0, D // 2048, body, jnp.zeros((2 * TOK, width), F32))
        qb[pair, :, lanes] = total.astype(BF)

    def keys_values(pair, half):
        lanes = pl.ds(0, 256) if half is None else pl.ds(half * HD, HD)

        def body(u, carry):
            rows = encz[pl.ds(4 * u, 4)].reshape(512, ENC)
            keys = jnp.dot(rows, wkb[pair, :, lanes], preferred_element_type=F32)
            kb[pl.ds(2 * u, 2), :, lanes] = keys.astype(BF).reshape(2, 256, -1)
            values = jnp.dot(rows, wvb[pair, :, lanes], preferred_element_type=F32)
            vb[pl.ds(2 * u, 2), :, lanes] = values.astype(BF).reshape(2, 256, -1)
            return carry

        lax.fori_loop(0, 2, body, 0)

    row_id = lax.broadcasted_iota(jnp.int32, (TOK, 256), 0)
    in_b = jnp.logical_and(row_id >= SPAN - 1, row_id < TOK - 1)
    blank = jnp.logical_and(lax.broadcasted_iota(jnp.int32, (TOK, HD), 0) < SPAN - 1, z == 0)

    def attend(pair, half, dst):
        halves = (0, 1) if half is None else (half,)
        for s in range(2):
            for h in halves:
                lanes = pl.ds(h * HD, HD)
                q = qb[pair, s * TOK : (s + 1) * TOK, lanes]
                ka, kb_ = kb[2 * s, :, lanes], kb[2 * s + 1, :, lanes]
                dims = (((1,), (1,)), ((), ()))
                sa_ = lax.dot_general(q, ka, dims, preferred_element_type=F32)
                sb_ = lax.dot_general(q, kb_, dims, preferred_element_type=F32)
                scores = jnp.where(in_b, sb_, sa_) * F32(1.0 / math.sqrt(HD))
                peak = jnp.max(scores, axis=1, keepdims=True)
                e = jnp.exp(scores - peak)
                total = jnp.sum(e, axis=1, keepdims=True)
                wa = jnp.where(in_b, 0.0, e).astype(BF)
                wb = jnp.where(in_b, e, 0.0).astype(BF)
                o = jnp.dot(wa, vb[2 * s, :, lanes], preferred_element_type=F32)
                o = o + jnp.dot(wb, vb[2 * s + 1, :, lanes], preferred_element_type=F32)
                o = jnp.where(blank, 0.0, o / total)
                dst[s * TOK : (s + 1) * TOK, lanes] = o.astype(BF)

    def add_out(pair, is_first):
        def body(k, carry):
            cols = pl.ds(pl.multiple_of(k * OUT_CHUNK, OUT_CHUNK), OUT_CHUNK)
            term = jnp.dot(att[...], wob[pair, :, cols], preferred_element_type=F32)
            acc[:, cols] = term if is_first else acc[:, cols] + term
            return carry

        lax.fori_loop(0, D // OUT_CHUNK, body, 0)

    step(0, 0)
    step(1, 0)
    step(2, 0)
    step(3, 0)
    z_wait(1, KV)
    z_start(2, KV)
    step(4, 0)
    step(5, 0)
    step(6, 0)
    step(0, 1)
    z_wait(1, Q0)
    z_start(2, Q0)
    step(1, 1)
    tok_x.wait_recv()
    local[2].wait()
    project(0, 0)
    e2_start(0)
    step(2, 1)
    e2_start(1)
    e2_start(2)
    z_wait(2, KV)
    z_start(3, KV)
    step(3, 1)
    z_wait(2, Q0)
    z_start(3, Q0)
    step(0, 2)
    step(1, 2)
    step(4, 1)
    step(2, 2)
    step(5, 1)
    step(0, 3)
    step(1, 3)
    project(1, None)
    step(3, 2)
    step(6, 1)
    e3_start(0)
    e3_start(1)
    e3_start(2)
    for part in range(len(E_COLS)):
        e3_copy(part).wait_recv()
    local[3].wait()
    local[4].wait()
    local[5].wait()
    whole(ask_r.at[pl.ds(0, NP - 1)], es.at[0]).wait()
    whole(send_e.at[pl.ds(0, NP - 1)], es.at[2]).wait()
    tail_in.wait_send()
    tok_x.wait_send()
    step(2, 3)
    z_wait(3, KV)
    z_start(4, KV)
    keys_values(0, 0)
    attend(0, 0, att0)
    keys_values(1, None)
    step(4, 2)
    attend(1, None, att)
    add_out(1, True)
    z_wait(3, Q0)
    z_start(4, Q0)
    step(3, 3)
    project(2, None)
    keys_values(2, None)
    step(5, 2, 0)
    step(6, 2, 0)
    step(5, 2, 1)
    attend(2, None, att)
    add_out(2, False)
    step(4, 3)
    step(6, 2, 1)
    step(5, 3, 0)
    project(3, None)
    keys_values(3, None)
    attend(3, None, att)
    z_wait(4, KV)
    keys_values(0, 1)
    step(6, 3, 0)
    z_wait(4, Q0)
    project(0, 1)
    attend(0, 1, att0)
    step(5, 3, 1)
    step(6, 3, 1)

    def last(k, carry):
        cols = pl.ds(pl.multiple_of(k * OUT_CHUNK, OUT_CHUNK), OUT_CHUNK)
        term = acc[:, cols] + jnp.dot(att[...], wob[3, :, cols], preferred_element_type=F32)
        term = term + jnp.dot(att0[...], wob[0, :, cols], preferred_element_type=F32)
        term = term.astype(BF)
        edge15 = lax.broadcasted_iota(jnp.int32, (16, OUT_CHUNK), 0) == 15
        for s, buf in enumerate((t_own, t_send)):
            edge = term[(s + 1) * TOK - 16 : (s + 1) * TOK]
            buf[0 : TOK - 16, cols] = term[s * TOK : (s + 1) * TOK - 16]
            buf[TOK - 16 : TOK, cols] = jnp.where(edge15, jnp.zeros_like(edge), edge)
            r_out[s, :, cols] = edge
        remote(t_send.at[:, cols], o_in.at[:, cols], st.at[3], rt.at[3], other).start()
        top = pl.ds(0, TOK - 16)
        pltpu.make_async_copy(t_own.at[top, cols], o_own.at[top, cols], l_sem.at[7]).start()
        return carry

    lax.fori_loop(0, D // OUT_CHUNK, last, 0)
    edges = []
    for i, dev in ((1, zdn), (2, odn)):
        fold(r_out[i - 1], i)
        edges.append(remote(e_out.at[i], e_in.at[i], st.at[i + 3], rt.at[i + 3], dev))
        edges[-1].start()
    whole(send_z.at[pl.ds(0, NZ - 1)], es.at[4]).wait()
    whole(encz.at[pl.ds(0, 4)], es.at[6]).wait()
    for k in range(1, 4):
        for part in (SL, KV, Q0):
            drain(sz.at[k - 1, part], z_units(k, part))
    for t in range(6):
        drain(sx.at[t], 15 * (QU + OU))
    for part in (SL, KV, Q0):
        drain(sz.at[3, part], z_units(4, part))
    drain(sx.at[6], 15 * (QU + OU))
    for edge in edges:
        edge.wait_recv()
    unfold(e_in[1].astype(F32) + e_in[2].astype(F32), t_own)
    bottom = pltpu.make_async_copy(t_own.at[last16], o_own.at[last16], l_sem.at[6])
    bottom.start()
    whole(t_own.at[pl.ds(0, TOK - 16)], l_sem.at[7]).wait()
    for edge in edges:
        edge.wait_send()
    whole(t_send, st.at[3]).wait()
    whole(o_in, rt.at[3]).wait()
    bottom.wait()


def fused(tokens, w_query, w_key, w_value, w_out, encoded, nbr_shard, nbr_row):
    any_ = pl.BlockSpec(memory_space=pl.ANY)
    vmem = pl.BlockSpec(memory_space=pltpu.VMEM)
    smem = pl.BlockSpec(memory_space=pltpu.SMEM)
    dma = pltpu.SemaphoreType.DMA
    V = pltpu.VMEM
    return pl.pallas_call(
        kernel,
        out_shape=(jax.ShapeDtypeStruct((TOK, D), BF), jax.ShapeDtypeStruct((TOK, D), BF)),
        in_specs=[any_] * 6 + [vmem, vmem, smem],
        out_specs=(any_, any_),
        scratch_shapes=[
            V((2 * TOK, D), BF),
            V((3, 16, 256), BF),
            V((3, 16, 256), BF),
            V((4, D, 256), BF),
            V((4, ENC, 256), BF),
            V((4, ENC, 256), BF),
            V((4, 256, D), BF),
            V((16, ROWS, ENC), BF),
            V((8, 128), jnp.int32),
            V((NP, 8, 128), jnp.int32),
            V((32, 8, 128), jnp.int32),
            V((2 * NP, 1, 128), jnp.int32),
            pltpu.SMEM((2 * NP, 1, 128), jnp.int32),
            V((NP, 2, ROWS, ENC), BF),
            V((2 * NP, ROWS, E_COLS[0][1]), BF),
            V((2 * NP, ROWS, E_COLS[1][1]), BF),
            V((2 * NP, ROWS, E_COLS[2][1]), BF),
            V((NZ, 4, ROWS, ENC), BF),
            V((8, 128, ENC), BF),
            V((4, 2 * TOK, 256), BF),
            V((4, 256, 256), BF),
            V((4, 256, 256), BF),
            V((2 * TOK, 256), BF),
            V((2 * TOK, 256), BF),
            V((2 * TOK, D), F32),
            V((TOK, D), BF),
            V((TOK, D), BF),
            V((2, 16, D), BF),
            dma((8,)),
            dma((4, 3)),
            dma((4, 3)),
            dma((7,)),
            dma((2, 7, 4)),
            dma((7,)),
            dma((len(E_COLS),)),
            dma((len(E_COLS),)),
            dma((len(E_COLS),)),
            dma((6,)),
            dma((6,)),
        ],
        compiler_params=pltpu.CompilerParams(
            collective_id=0, has_side_effects=True, vmem_limit_bytes=56 * 1024 * 1024
        ),
    )(tokens, w_query, w_key, w_value, w_out, encoded, nbr_shard, nbr_row, nbr_shard)


def shards(tokens, w_query, w_key, w_value, w_out, encoded, nbr_shard, nbr_row):
    own, received = fused(
        tokens, w_query, w_key, w_value, w_out, encoded, nbr_shard.T, nbr_row.T
    )
    return (own.astype(F32) + received.astype(F32)).astype(BF)


def solution(mesh):
    return jax.shard_map(
        shards,
        mesh=mesh,
        in_specs=(
            P(("dp", "mp"), None),
            P(None, "mp"),
            P(None, "mp"),
            P(None, "mp"),
            P("mp", None),
            P("dp", None, None),
            P("dp", None),
            P("dp", None),
        ),
        out_specs=P(("dp", "mp"), None),
        check_vma=False,
    )
```

```python
import math

import jax
import jax.numpy as jnp
from jax import lax
from jax.experimental import pallas as pl
from jax.experimental.pallas import tpu as pltpu
from jax.sharding import PartitionSpec as P

MESH = pl.DeviceIdType.MESH
BF = jnp.bfloat16
F32 = jnp.float32
HD = 128
SPAN = 64
D = 4096
ENC = 896
TOK = 128
NX = 4
NZ = 8
NP = 32
ROWS = 16
E_COLS = ((0, 384), (384, 256), (640, 256))
QZ = 1024
QSPLIT = 288
QU = (D - QZ) // 16
OU = D // 16
SLOTS = ((1, 0), (1, 1), (2, 0), (2, 1), (3, 0), (3, 1), (0, 1))
OUT_CHUNK = 2048


def kernel(
    tok, wq, wk, wv, wo, enc, nbr_v, row_v, nbr_s, o_own, o_in,
    tokv, e_out, e_in, wqb, wkb, wvb, wob, band, ask_o, ask_r, rank_v, pick_v, pick_s, send_e, recv_a, recv_b, recv_c, send_z, encz,
    qb, kb, vb, att, att0, acc, t_own, t_send, r_out,
    l_sem, sz, rz, sx, rx, es, e1r, e2r, e3r, st, rt,
):
    d = lax.axis_index("dp")
    z = lax.axis_index("mp")
    x = d // 8
    y = lax.rem(d // 2, 4)
    c = lax.rem(d, 2)
    other = (d + 1 - 2 * c, z)
    zdn = (d, lax.rem(z + 7, NZ))
    zup = (d, lax.rem(z + 1, NZ))
    odn = (other[0], zdn[1])
    oup = (other[0], zup[1])

    def plane(px, py):
        return (px * 8 + py * 2 + c, z)

    ring = {
        "x": (plane(lax.rem(x + 1, 4), y), plane(lax.rem(x + 3, 4), y)),
        "y": (plane(x, lax.rem(y + 1, 4)), plane(x, lax.rem(y + 3, 4))),
    }
    cs = pl.ds(pl.multiple_of(c * HD, HD), HD)

    def remote(src, dst, ssem, rsem, dev):
        return pltpu.make_async_remote_copy(
            src_ref=src, dst_ref=dst, send_sem=ssem, recv_sem=rsem, device_id=dev, device_id_type=MESH
        )

    half0 = pl.ds(0, HD)
    local = [
        pltpu.make_async_copy(enc.at[:, pl.ds(pl.multiple_of(z * ROWS, ROWS), ROWS), :], band, l_sem.at[0]),
        pltpu.make_async_copy(tok, tokv.at[pl.ds(0, TOK)], l_sem.at[1]),
        pltpu.make_async_copy(wq.at[:, cs], wqb.at[0, :, half0], l_sem.at[2]),
        pltpu.make_async_copy(wk.at[:, cs], wkb.at[0, :, half0], l_sem.at[3]),
        pltpu.make_async_copy(wv.at[:, cs], wvb.at[0, :, half0], l_sem.at[4]),
        pltpu.make_async_copy(wo.at[cs, :], wob.at[0, half0, :], l_sem.at[5]),
    ]
    for copy in local:
        copy.start()

    bar = pltpu.get_barrier_semaphore()

    def greet_plane(k, carry):
        pl.semaphore_signal(bar, inc=1, device_id=(lax.rem(d + k, NP), z), device_id_type=MESH)
        return carry

    def greet_z(k, carry):
        pl.semaphore_signal(bar, inc=1, device_id=(d, lax.rem(z + k, NZ)), device_id_type=MESH)
        return carry

    lax.fori_loop(1, NP, greet_plane, 0)
    lax.fori_loop(1, NZ, greet_z, 0)
    pl.semaphore_signal(bar, inc=1, device_id=odn, device_id_type=MESH)
    pl.semaphore_signal(bar, inc=1, device_id=oup, device_id_type=MESH)
    pl.semaphore_wait(bar, NP - 1 + NZ - 1 + 2)

    q_slice = (y * 4 + x, x * 4 + y)
    o_slice = (x * 4 + y, y * 4 + x)

    def q_at(sl, start, size):
        if sl is None:
            return wq.at[pl.ds(start, size), cs]
        return wqb.at[sl[0], pl.ds(start, size), pl.ds(sl[1] * HD, HD)]

    def o_at(sl, start, size):
        if sl is None:
            return wo.at[cs, pl.ds(start, size)]
        return wob.at[sl[0], pl.ds(sl[1] * HD, HD), pl.ds(start, size)]

    def kv_at(arg, buf, sl):
        if sl is None:
            return arg.at[:, cs]
        return buf.at[sl[0], :, pl.ds(sl[1] * HD, HD)]

    def drain(sem, units):
        if units <= D:
            ref = wqb.at[0, pl.ds(0, units), pl.ds(0, HD)]
        else:
            ref = wqb.at[pl.ds(0, 2), pl.ds(0, units // 2), pl.ds(0, HD)]
        pltpu.make_async_copy(ref, ref, sem).wait()

    SL, KV, Q0 = 0, 1, 2

    def z_start(k, part):
        for way in (0, 1):
            src_sl = None if k == 1 else (k - 1, way)
            dst_sl = (k, way) if k < 4 else (0, 1)
            pairs = []
            if part == SL and (k < 4 or way == 0):
                start = pl.multiple_of(QZ + q_slice[way] * QU, 16)
                pairs.append((q_at(src_sl, start, QU), q_at(dst_sl, start, QU)))
                start = pl.multiple_of(o_slice[way] * OU, 128)
                pairs.append((o_at(src_sl, start, OU), o_at(dst_sl, start, OU)))
            elif part == KV:
                if k < 4 or way == 0:
                    pairs.append((kv_at(wk, wkb, src_sl), kv_at(wk, wkb, dst_sl)))
                if k < 4 or way == 1:
                    pairs.append((kv_at(wv, wvb, src_sl), kv_at(wv, wvb, dst_sl)))
            elif part == Q0:
                start, size = (0, QZ) if k < 4 else ((0, QSPLIT) if way == 0 else (QSPLIT, QZ - QSPLIT))
                pairs.append((q_at(src_sl, start, size), q_at(dst_sl, start, size)))
            for src, dst in pairs:
                remote(src, dst, sz.at[k - 1, part], rz.at[k - 1, part], zup if way else zdn).start()

    def z_units(k, part):
        units = {SL: QU + OU, KV: 2 * ENC, Q0: QZ}[part]
        return 2 * units if k < 4 else units

    def z_wait(k, part):
        drain(rz.at[k - 1, part], z_units(k, part))

    def view(arr, sl, start, size):
        if arr == 0:
            return q_at(sl, pl.multiple_of(QZ + start, 16), size)
        return o_at(sl, pl.multiple_of(start, 128), size)

    def x_start(t, phase, arr):
        sl = SLOTS[t]
        u = (QU, OU)[arr]
        x_first = (arr == 0) == (t % 2 == 0)
        i1, i2 = (x, y) if x_first else (y, x)
        up, dn = ring["x" if x_first == (phase < 2) else "y"]
        if phase == 0:
            spans = [((i2 * 4 + i1) * u, u)] * 2
        elif phase == 1:
            spans = [
                ((i2 * 4 + lax.rem(i1 + 3, 4)) * u, u // 2),
                ((i2 * 4 + lax.rem(i1 + 1, 4)) * u + u // 2, u // 2),
            ]
        elif phase == 2:
            spans = [(i2 * 4 * u, 4 * u)] * 2
        else:
            spans = [
                (lax.rem(i2 + 3, 4) * 4 * u, 2 * u),
                (lax.rem(i2 + 1, 4) * 4 * u + 2 * u, 2 * u),
            ]
        for way, dev in enumerate((up, dn)):
            ref = view(arr, sl, *spans[way])
            remote(ref, ref, sx.at[t], rx.at[arr, t, phase], dev).start()

    def x_wait(t, phase, arr):
        drain(rx.at[arr, t, phase], 2 * (QU, OU)[arr] * (2, 1, 8, 4)[phase] // 2)

    def ph1(t):
        for arr in (0, 1):
            x_start(t, 0, arr)

    def step(t, phase, only=None):
        for arr in (0, 1) if only is None else (only,):
            x_wait(t, phase, arr)
            if phase < 3:
                x_start(t, phase + 1, arr)

    z_start(1, SL)
    last16 = pl.ds(TOK - 16, 16)
    is15 = lax.broadcasted_iota(jnp.int32, (16, 256), 0) == 15

    def fold(rows, i):
        row = rows.astype(F32)[15:16, :]
        packed = jnp.zeros((16, 256), F32)
        for j in range(16):
            piece = jnp.broadcast_to(row[:, 256 * j : 256 * (j + 1)], (16, 256))
            packed = jnp.where(lax.broadcasted_iota(jnp.int32, (16, 256), 0) == j, piece, packed)
        e_out[i] = packed.astype(BF)

    def unfold(packed, buf):
        for j in range(16):
            cols = pl.ds(256 * j, 256)
            piece = jnp.broadcast_to(packed[j : j + 1, :], (16, 256))
            buf[TOK - 16 : TOK, cols] = jnp.where(is15, piece, buf[TOK - 16 : TOK, cols].astype(F32)).astype(BF)

    def each(n, f):
        def body(k, carry):
            f(k)
            return carry

        lax.fori_loop(1, n, body, 0)

    def whole(ref, sem):
        return pltpu.make_async_copy(ref, ref, sem)

    ask_o[...] = jnp.full((8, 128), -16, jnp.int32)
    ask_o[0:2, 0:16] = nbr_v[...] * 16 + row_v[...]

    def ask_copy(k):
        p = lax.rem(d + k, NP)
        remote(ask_o, ask_r.at[d], es.at[0], es.at[1], (p, z)).start()

    each(NP, ask_copy)
    z_start(1, KV)
    z_start(1, Q0)
    local[1].wait()
    fold(tokv[TOK - 16 : TOK, :], 0)
    tail_in = remote(e_out.at[0], e_in.at[0], st.at[0], rt.at[0], zup)
    tail_in.start()
    ask_r[pl.ds(d, 1)] = ask_o[...][None]
    place = 2 * lax.broadcasted_iota(jnp.int32, (8, 128), 1) + lax.broadcasted_iota(jnp.int32, (8, 128), 0)
    mine = lax.shift_right_arithmetic(ask_o[...], 4)
    for f in range(32):
        same = jnp.logical_and(mine == nbr_s[f % 2, f // 2], place < f)
        rank_v[f] = jnp.where(same, 1, 0)
    rank = jnp.max(jnp.max(rank_v[...], axis=1, keepdims=True), axis=2, keepdims=True)
    pick_v[NP:, :, :] = jnp.broadcast_to(rank, (32, 1, 128))
    z_wait(1, SL)
    z_start(2, SL)
    ph1(0)
    ph1(1)
    local[0].wait()
    whole(ask_r.at[pl.ds(0, NP - 1)], es.at[1]).wait()
    codes = ask_r[...]
    hit = lax.shift_right_arithmetic(codes, 4) == d
    key = place[None] * 16 + jnp.bitwise_and(codes, 15)
    low = jnp.where(hit, key, 1 << 20)
    low = jnp.min(jnp.min(low, axis=1, keepdims=True), axis=2, keepdims=True)
    high = jnp.where(hit, key, 0)
    high = jnp.max(jnp.max(high, axis=1, keepdims=True), axis=2, keepdims=True)
    lane = lax.broadcasted_iota(jnp.int32, (NP, 1, 128), 2)
    pick_v[:NP, :, :] = jnp.bitwise_and(jnp.where(lane == 0, low, high), 15)
    to_smem = pltpu.make_async_copy(pick_v, pick_s, l_sem.at[6])
    to_smem.start()
    to_smem.wait()

    recv_e = (recv_a, recv_b, recv_c)

    def e1_start(part):
        cols = pl.ds(*E_COLS[part])

        def pick(s, carry):
            for j in range(2):
                send_e[s, j, :, cols] = band[pick_s[s, 0, j], :, cols]
            return carry

        lax.fori_loop(0, NP, pick, 0)

        def copy(k):
            p = lax.rem(d + k, NP)
            remote(
                send_e.at[p, :, :, cols], recv_e[part].at[pl.ds(2 * d, 2)], es.at[2], e1r.at[part], (p, z)
            ).start()

        each(NP, copy)
        recv_e[part][pl.ds(2 * d, 2)] = send_e[d, :, :, cols]

    my_rows = pl.ds(pl.multiple_of(z * ROWS, ROWS), ROWS)

    def e2_start(part):
        cols = pl.ds(*E_COLS[part])
        whole(recv_e[part].at[pl.ds(0, 2 * NP - 2)], e1r.at[part]).wait()

        def pick(mz, carry):
            spans = (lax.rem(2 * mz + 15, 16), 2 * mz)
            for i in range(4):
                span, n = spans[i // 2], i % 2
                place = 2 * nbr_s[n, span] + pick_s[NP + 2 * span + n, 0, 0]
                send_z[mz, i, :, cols] = recv_e[part][place]
            return carry

        lax.fori_loop(0, NZ, pick, 0)

        def copy(k):
            p = lax.rem(z + k, NZ)
            remote(
                send_z.at[p, :, :, cols], encz.at[pl.ds(0, 4), my_rows, cols], es.at[4], e2r.at[part], (d, p)
            ).start()

        each(NZ, copy)
        encz[pl.ds(0, 4), my_rows, cols] = send_z[z, :, :, cols]

    def e3_copy(part):
        cols = pl.ds(*E_COLS[part])
        return remote(encz.at[pl.ds(0, 4), :, cols], encz.at[pl.ds(4, 4), :, cols], es.at[6], e3r.at[part], other)

    def e3_start(part):
        cols = pl.ds(*E_COLS[part])
        whole(send_z.at[pl.ds(0, NZ - 1), :, :, cols], e2r.at[part]).wait()
        e3_copy(part).start()

    for part in range(len(E_COLS)):
        e1_start(part)

    tail_in.wait_recv()
    unfold(e_in[0].astype(F32), tokv)
    tok_x = remote(tokv.at[pl.ds(0, TOK)], tokv.at[pl.ds(TOK, TOK)], st.at[1], rt.at[1], other)
    tok_x.start()
    z_wait(2, SL)
    z_start(3, SL)
    ph1(2)
    ph1(3)
    z_wait(3, SL)
    z_start(4, SL)
    ph1(4)
    ph1(5)
    z_wait(4, SL)
    ph1(6)

    def project(pair, half):
        lanes = pl.ds(0, 256) if half is None else pl.ds(half * HD, HD)
        width = 256 if half is None else HD

        def body(k, total):
            start = pl.multiple_of(k * D, D)
            return total + jnp.dot(
                tokv[:, pl.ds(start, D)], wqb[pair, pl.ds(start, D), lanes], preferred_element_type=F32
            )

        total = lax.fori_loop(0, 1, body, jnp.zeros((2 * TOK, width), F32))
        qb[pair, :, lanes] = total.astype(BF)

    def keys_values(pair, half):
        lanes = pl.ds(0, 256) if half is None else pl.ds(half * HD, HD)

        def body(u, carry):
            rows = encz[pl.ds(4 * u, 4)].reshape(512, ENC)
            keys = jnp.dot(rows, wkb[pair, :, lanes], preferred_element_type=F32)
            kb[pl.ds(2 * u, 2), :, lanes] = keys.astype(BF).reshape(2, 256, -1)
            values = jnp.dot(rows, wvb[pair, :, lanes], preferred_element_type=F32)
            vb[pl.ds(2 * u, 2), :, lanes] = values.astype(BF).reshape(2, 256, -1)
            return carry

        lax.fori_loop(0, 2, body, 0)

    row_id = lax.broadcasted_iota(jnp.int32, (TOK, 256), 0)
    in_b = jnp.logical_and(row_id >= SPAN - 1, row_id < TOK - 1)
    blank = jnp.logical_and(lax.broadcasted_iota(jnp.int32, (TOK, HD), 0) < SPAN - 1, z == 0)

    def attend(pair, half, dst):
        halves = (0, 1) if half is None else (half,)
        for s in range(2):
            for h in halves:
                lanes = pl.ds(h * HD, HD)
                q = qb[pair, s * TOK : (s + 1) * TOK, lanes]
                ka, kb_ = kb[2 * s, :, lanes], kb[2 * s + 1, :, lanes]
                dims = (((1,), (1,)), ((), ()))
                sa_ = lax.dot_general(q, ka, dims, preferred_element_type=F32)
                sb_ = lax.dot_general(q, kb_, dims, preferred_element_type=F32)
                scores = jnp.where(in_b, sb_, sa_) * F32(1.0 / math.sqrt(HD))
                peak = jnp.max(scores, axis=1, keepdims=True)
                e = jnp.exp(scores - peak)
                total = jnp.sum(e, axis=1, keepdims=True)
                wa = jnp.where(in_b, 0.0, e).astype(BF)
                wb = jnp.where(in_b, e, 0.0).astype(BF)
                o = jnp.dot(wa, vb[2 * s, :, lanes], preferred_element_type=F32)
                o = o + jnp.dot(wb, vb[2 * s + 1, :, lanes], preferred_element_type=F32)
                o = jnp.where(blank, 0.0, o / total)
                dst[s * TOK : (s + 1) * TOK, lanes] = o.astype(BF)

    def add_out(pair, is_first):
        def body(k, carry):
            cols = pl.ds(pl.multiple_of(k * OUT_CHUNK, OUT_CHUNK), OUT_CHUNK)
            term = jnp.dot(att[...], wob[pair, :, cols], preferred_element_type=F32)
            acc[:, cols] = term if is_first else acc[:, cols] + term
            return carry

        lax.fori_loop(0, D // OUT_CHUNK, body, 0)

    step(0, 0)
    step(1, 0)
    step(2, 0)
    step(3, 0)
    z_wait(1, KV)
    z_start(2, KV)
    step(4, 0)
    step(5, 0)
    step(6, 0)
    step(0, 1)
    z_wait(1, Q0)
    z_start(2, Q0)
    step(1, 1)
    tok_x.wait_recv()
    local[2].wait()
    project(0, 0)
    e2_start(0)
    step(2, 1)
    e2_start(1)
    e2_start(2)
    z_wait(2, KV)
    z_start(3, KV)
    step(3, 1)
    z_wait(2, Q0)
    z_start(3, Q0)
    step(0, 2)
    step(1, 2)
    step(4, 1)
    step(2, 2)
    step(5, 1)
    step(0, 3)
    step(1, 3)
    project(1, None)
    step(3, 2)
    step(6, 1)
    e3_start(0)
    e3_start(1)
    e3_start(2)
    for part in range(len(E_COLS)):
        e3_copy(part).wait_recv()
    local[3].wait()
    local[4].wait()
    local[5].wait()
    whole(ask_r.at[pl.ds(0, NP - 1)], es.at[0]).wait()
    whole(send_e.at[pl.ds(0, NP - 1)], es.at[2]).wait()
    tail_in.wait_send()
    tok_x.wait_send()
    step(2, 3)
    z_wait(3, KV)
    z_start(4, KV)
    keys_values(0, 0)
    attend(0, 0, att0)
    keys_values(1, None)
    step(4, 2)
    attend(1, None, att)
    add_out(1, True)
    z_wait(3, Q0)
    z_start(4, Q0)
    step(3, 3)
    project(2, None)
    keys_values(2, None)
    step(5, 2, 0)
    step(6, 2, 0)
    step(5, 2, 1)
    attend(2, None, att)
    add_out(2, False)
    step(4, 3)
    step(6, 2, 1)
    step(5, 3, 0)
    project(3, None)
    keys_values(3, None)
    attend(3, None, att)
    z_wait(4, KV)
    keys_values(0, 1)
    step(6, 3, 0)
    z_wait(4, Q0)
    project(0, 1)
    attend(0, 1, att0)
    step(5, 3, 1)
    step(6, 3, 1)

    def last(k, carry):
        cols = pl.ds(pl.multiple_of(k * OUT_CHUNK, OUT_CHUNK), OUT_CHUNK)
        term = acc[:, cols] + jnp.dot(att[...], wob[3, :, cols], preferred_element_type=F32)
        term = term + jnp.dot(att0[...], wob[0, :, cols], preferred_element_type=F32)
        term = term.astype(BF)
        edge15 = lax.broadcasted_iota(jnp.int32, (16, OUT_CHUNK), 0) == 15
        for s, buf in enumerate((t_own, t_send)):
            edge = term[(s + 1) * TOK - 16 : (s + 1) * TOK]
            buf[0 : TOK - 16, cols] = term[s * TOK : (s + 1) * TOK - 16]
            buf[TOK - 16 : TOK, cols] = jnp.where(edge15, jnp.zeros_like(edge), edge)
            r_out[s, :, cols] = edge
        remote(t_send.at[:, cols], o_in.at[:, cols], st.at[3], rt.at[3], other).start()
        top = pl.ds(0, TOK - 16)
        pltpu.make_async_copy(t_own.at[top, cols], o_own.at[top, cols], l_sem.at[7]).start()
        return carry

    lax.fori_loop(0, D // OUT_CHUNK, last, 0)
    edges = []
    for i, dev in ((1, zdn), (2, odn)):
        fold(r_out[i - 1], i)
        edges.append(remote(e_out.at[i], e_in.at[i], st.at[i + 3], rt.at[i + 3], dev))
        edges[-1].start()
    whole(send_z.at[pl.ds(0, NZ - 1)], es.at[4]).wait()
    whole(encz.at[pl.ds(0, 4)], es.at[6]).wait()
    for k in range(1, 4):
        for part in (SL, KV, Q0):
            drain(sz.at[k - 1, part], z_units(k, part))
    for t in range(6):
        drain(sx.at[t], 15 * (QU + OU))
    for part in (SL, KV, Q0):
        drain(sz.at[3, part], z_units(4, part))
    drain(sx.at[6], 15 * (QU + OU))
    for edge in edges:
        edge.wait_recv()
    unfold(e_in[1].astype(F32) + e_in[2].astype(F32), t_own)
    bottom = pltpu.make_async_copy(t_own.at[last16], o_own.at[last16], l_sem.at[6])
    bottom.start()
    whole(t_own.at[pl.ds(0, TOK - 16)], l_sem.at[7]).wait()
    for edge in edges:
        edge.wait_send()
    whole(t_send, st.at[3]).wait()
    whole(o_in, rt.at[3]).wait()
    bottom.wait()


def fused(tokens, w_query, w_key, w_value, w_out, encoded, nbr_shard, nbr_row):
    any_ = pl.BlockSpec(memory_space=pl.ANY)
    vmem = pl.BlockSpec(memory_space=pltpu.VMEM)
    smem = pl.BlockSpec(memory_space=pltpu.SMEM)
    dma = pltpu.SemaphoreType.DMA
    V = pltpu.VMEM
    return pl.pallas_call(
        kernel,
        out_shape=(jax.ShapeDtypeStruct((TOK, D), BF), jax.ShapeDtypeStruct((TOK, D), BF)),
        in_specs=[any_] * 6 + [vmem, vmem, smem],
        out_specs=(any_, any_),
        scratch_shapes=[
            V((2 * TOK, D), BF),
            V((3, 16, 256), BF),
            V((3, 16, 256), BF),
            V((4, D, 256), BF),
            V((4, ENC, 256), BF),
            V((4, ENC, 256), BF),
            V((4, 256, D), BF),
            V((16, ROWS, ENC), BF),
            V((8, 128), jnp.int32),
            V((NP, 8, 128), jnp.int32),
            V((32, 8, 128), jnp.int32),
            V((2 * NP, 1, 128), jnp.int32),
            pltpu.SMEM((2 * NP, 1, 128), jnp.int32),
            V((NP, 2, ROWS, ENC), BF),
            V((2 * NP, ROWS, E_COLS[0][1]), BF),
            V((2 * NP, ROWS, E_COLS[1][1]), BF),
            V((2 * NP, ROWS, E_COLS[2][1]), BF),
            V((NZ, 4, ROWS, ENC), BF),
            V((8, 128, ENC), BF),
            V((4, 2 * TOK, 256), BF),
            V((4, 256, 256), BF),
            V((4, 256, 256), BF),
            V((2 * TOK, 256), BF),
            V((2 * TOK, 256), BF),
            V((2 * TOK, D), F32),
            V((TOK, D), BF),
            V((TOK, D), BF),
            V((2, 16, D), BF),
            dma((8,)),
            dma((4, 3)),
            dma((4, 3)),
            dma((7,)),
            dma((2, 7, 4)),
            dma((7,)),
            dma((len(E_COLS),)),
            dma((len(E_COLS),)),
            dma((len(E_COLS),)),
            dma((6,)),
            dma((6,)),
        ],
        compiler_params=pltpu.CompilerParams(
            collective_id=0, has_side_effects=True, vmem_limit_bytes=56 * 1024 * 1024
        ),
    )(tokens, w_query, w_key, w_value, w_out, encoded, nbr_shard, nbr_row, nbr_shard)


def shards(tokens, w_query, w_key, w_value, w_out, encoded, nbr_shard, nbr_row):
    own, received = fused(
        tokens, w_query, w_key, w_value, w_out, encoded, nbr_shard.T, nbr_row.T
    )
    return (own.astype(F32) + received.astype(F32)).astype(BF)


def solution(mesh):
    return jax.shard_map(
        shards,
        mesh=mesh,
        in_specs=(
            P(("dp", "mp"), None),
            P(None, "mp"),
            P(None, "mp"),
            P(None, "mp"),
            P("mp", None),
            P("dp", None, None),
            P("dp", None),
            P("dp", None),
        ),
        out_specs=P(("dp", "mp"), None),
        check_vma=False,
    )
```
